128 devices in a mesh: row: 8 (over x_hi, y), col: 16 (over z, x_lo, core).
Axes of the slice: x: 4 (x_hi: 2, x_lo: 2; x = x_hi * 2 + x_lo), y: 4, z: 4, core: 2. Of those that a mesh axis runs over, the one named last changes fastest.
Arguments:
- grad_out: bfloat16 [16384, 8192], P('col', 'row'), may hold values from -4 to 4
- proj_weight: bfloat16 [8192, 4096], P('col', 'row'), may hold values from -0.09375 to 0.09375
- queries: bfloat16 [16384, 4096], P('col', 'row'), may hold values from -5 to 5
- keys: bfloat16 [16384, 4096], P('col', 'row'), may hold values from -5 to 5
- values: bfloat16 [16384, 4096], P('col', 'row'), may hold values from -6 to 6
- cache_keys: bfloat16 [1024, 4096], P('col', 'row'), may hold values from -6 to 6
- cache_values: bfloat16 [1024, 4096], P('col', 'row'), may hold values from -6 to 6
- block_table: int32 [128, 4], P('col'), may hold values from 0 to 7, all different within a row
Outputs:
- grad_q: bfloat16 [16384, 4096], P('col', 'row')
- grad_k: bfloat16 [16384, 4096], P('col', 'row')
- grad_v: bfloat16 [16384, 4096], P('col', 'row')
- grad_cache_k: float32 [1024, 4096], P('col', 'row')
- grad_cache_v: float32 [1024, 4096], P('col', 'row')
- grad_weight: bfloat16 [8192, 4096], P('col', 'row')
The draws below stay inside these ranges and needn't reach their ends.
Inputs may be any that keep to these rules, and one draw needn't show every extreme that they name: `block_table`: each row names 4 different cached blocks, and every cached block is named by some row.
All inputs are finite; a program needn't handle non-finite values.
Results may differ from the reference program's by a relative error of at most 0.023.
Values may be sent and summed in bfloat16 or wider, within the bound.
No kernel may reach another device: no remote copies, remote signals or barrier semaphores. Data moves between devices by JAX's collectives and lax.ppermute only.
A program may use at most 128 MiB of HBM per device.

```python
import math
import jax
import jax.numpy as jnp
from jax import lax

D = 8192
HEADS = 32
HEAD_DIM = 128
BLOCK = 128
CB = 8
KB = 4
TOKENS = 16384
CACHE = 1024
QBLOCKS = 128
N_COL = 16


def normal_field(first_key, second_key, spread):
    entries = jax.random.normal(first_key, (TOKENS, HEADS * HEAD_DIM), jnp.float32)
    row_scale = jnp.exp(jax.random.uniform(second_key, (TOKENS, 1), jnp.float32, -spread, spread))
    return jnp.clip(entries * row_scale, -5.0, 5.0)


def draw_queries(key, part):
    key = jax.random.fold_in(key, 1)
    first_key, second_key = jax.random.split(key)
    return normal_field(first_key, second_key, 0.8).astype(jnp.bfloat16)


def draw_keys(key, part):
    key = jax.random.fold_in(key, 2)
    first_key, second_key = jax.random.split(key)
    return normal_field(first_key, second_key, 0.8).astype(jnp.bfloat16)


def raised(values, stream_key, source, target, blocks, factor):
    owner, partner = [(jnp.arange(values.shape[dim]) // (values.shape[dim] // blocks)).reshape([-1 if axis == dim else 1 for axis in range(values.ndim)]) for dim in (source, target)]
    chosen = jax.random.permutation(stream_key, blocks)[partner]
    strong = (owner == chosen) | (owner == (partner + blocks // 2) % blocks)
    return jnp.where(strong, factor * values, values)


def steps_of(key, extent, pieces, smallest, top_value):
    level, own = 1.0, jax.random.fold_in(key, 6)
    for dim, parts in pieces:
        draws = jnp.exp(jax.random.uniform(jax.random.fold_in(own, dim), (parts,), jnp.float32, smallest / len(pieces), top_value / len(pieces)))
        level = level * jnp.repeat(draws, extent[dim] // parts).reshape([-1 if axis == dim else 1 for axis in range(len(extent))])
    return level


def different_ones(own_key, rows, amount, top, lift):
    order = jax.random.permutation(jax.random.fold_in(own_key, 1), amount)
    favour = order
    for power in range(3):
        favour = favour * favour // amount
    favour = favour * lift // amount
    chance = jax.random.randint(jax.random.fold_in(own_key, 2), (rows, amount), 0, 4096) + favour
    sure = jax.random.permutation(jax.random.fold_in(own_key, 3), rows)[jnp.arange(amount) % rows]
    chance = jnp.where(jnp.arange(rows)[:, None] == sure[None, :], 1 << 14, chance)
    score = chance * amount + jnp.arange(amount)
    return lax.top_k(score.astype(jnp.int32), top)[1].astype(jnp.int32)


def noise(own_key, dims, scale, bound, shards=(), held_as=jnp.bfloat16):
    result = scale * jax.random.normal(own_key, dims, jnp.float32)
    if shards:
        result = result * steps_of(own_key, dims, shards, -0.22, 0.18)
    return jnp.clip(result, -bound, bound).astype(held_as)


def bell_draw_with(key, extent, deviation, bound, shards, heavy, held_as=jnp.bfloat16):
    result = deviation * jax.random.normal(key, extent, jnp.float32)
    if shards:
        result = result * steps_of(key, extent, shards, -0.22, 0.18)
    return jnp.clip(raised(result, jax.random.fold_in(key, 3), *heavy), -bound, bound).astype(held_as)


def setup_inputs(seed: int = 0) -> dict:
    key_of = jax.random.split(jax.random.key(seed), 9)
    return {
        "grad_out": bell_draw_with(key_of[0], (TOKENS, D), 0.5, 4.0, ((0, 16), (1, 8)), (0, 1, 16, 2.0)),
        "proj_weight": noise(key_of[1], (D, HEADS * HEAD_DIM), (HEADS * HEAD_DIM) ** -0.5, 0.09375, ((0, 16), (1, 8))),
        "queries": draw_queries(jax.random.fold_in(key_of[8], 71), 0),
        "keys": draw_keys(jax.random.fold_in(key_of[8], 71), 0),
        "values": noise(key_of[4], (TOKENS, HEADS * HEAD_DIM), 1.0, 6.0, ((0, 16), (1, 8))),
        "cache_keys": noise(key_of[5], (CACHE, HEADS * HEAD_DIM), 1.0, 6.0, ((0, 16), (1, 8))),
        "cache_values": noise(key_of[6], (CACHE, HEADS * HEAD_DIM), 1.0, 6.0, ((0, 16), (1, 8))),
        "block_table": different_ones(key_of[7], QBLOCKS, CB, KB, 0),
    }


def rounded(array):
    return lax.optimization_barrier(array.astype(jnp.bfloat16))

def reference(grad_out, proj_weight, queries, keys, values, cache_keys, cache_values, block_table):
    width = HEADS * HEAD_DIM
    inverse_root = 1.0 / math.sqrt(HEAD_DIM)
    blocks = TOKENS // BLOCK
    grad_attn = rounded(jnp.dot(grad_out, proj_weight, preferred_element_type=jnp.float32))

    def split(array, count):
        return array.reshape(count, BLOCK, HEADS, HEAD_DIM)
    cache_key_blocks = split(cache_keys, CB)
    cache_value_blocks = split(cache_values, CB)
    positions = jnp.arange(BLOCK, dtype=jnp.int32)
    causal = positions[:, None] >= positions[None, :]
    allowed = jnp.concatenate([jnp.ones((BLOCK, KB * BLOCK), dtype=bool), causal], axis=1)

    def one_block(carry, inputs):
        grad_ck, grad_cv = carry
        query, own_keys, own_values, grad_block, chosen = inputs
        key_list = jnp.concatenate([cache_key_blocks[chosen].reshape(KB * BLOCK, HEADS, HEAD_DIM), own_keys], axis=0)
        value_list = jnp.concatenate([cache_value_blocks[chosen].reshape(KB * BLOCK, HEADS, HEAD_DIM), own_values], axis=0)
        query_f = query.astype(jnp.float32)
        key_f = key_list.astype(jnp.float32)
        value_f = value_list.astype(jnp.float32)
        grad_f = grad_block.astype(jnp.float32)
        scores = jnp.einsum('qhd,khd->hqk', query_f, key_f) * inverse_root
        scores = jnp.where(allowed[None], scores, -jnp.inf)
        row_max = lax.optimization_barrier(jnp.max(scores, axis=-1, keepdims=True))
        weights = jnp.exp(scores - row_max)
        probs = weights / lax.optimization_barrier(jnp.sum(weights, axis=-1, keepdims=True))
        probs_f = rounded(probs).astype(jnp.float32)
        attn_full = jnp.einsum('hqk,khd->qhd', probs_f, value_f)
        delta = lax.optimization_barrier(jnp.sum(grad_f * attn_full, axis=-1))
        grad_probs = jnp.einsum('qhd,khd->hqk', grad_f, value_f)
        grad_scores = probs * (grad_probs - jnp.transpose(delta)[:, :, None])
        scores_f = rounded(grad_scores).astype(jnp.float32)
        grad_query = jnp.einsum('hqk,khd->qhd', scores_f, key_f) * inverse_root
        grad_key_list = jnp.einsum('hqk,qhd->khd', scores_f, query_f) * inverse_root
        grad_value_list = jnp.einsum('hqk,qhd->khd', probs_f, grad_f)
        grad_ck = grad_ck.at[chosen].add(grad_key_list[:KB * BLOCK].reshape(KB, BLOCK, HEADS, HEAD_DIM))
        grad_cv = grad_cv.at[chosen].add(grad_value_list[:KB * BLOCK].reshape(KB, BLOCK, HEADS, HEAD_DIM))
        outputs = (grad_query.astype(jnp.bfloat16), grad_key_list[KB * BLOCK:].astype(jnp.bfloat16), grad_value_list[KB * BLOCK:].astype(jnp.bfloat16), attn_full.astype(jnp.bfloat16))
        return ((grad_ck, grad_cv), outputs)
    start_carry = (jnp.zeros((CB, BLOCK, HEADS, HEAD_DIM), jnp.float32), jnp.zeros((CB, BLOCK, HEADS, HEAD_DIM), jnp.float32))
    inputs = (split(queries, blocks), split(keys, blocks), split(values, blocks), split(grad_attn, blocks), block_table)
    (grad_ck, grad_cv), outputs = lax.scan(one_block, start_carry, inputs)
    grad_q = outputs[0].reshape(TOKENS, width)
    grad_k = outputs[1].reshape(TOKENS, width)
    grad_v = outputs[2].reshape(TOKENS, width)
    attn_out = outputs[3].reshape(TOKENS, width)
    group_rows = TOKENS // N_COL

    def add_group(total, index):
        rows_out = lax.dynamic_slice_in_dim(grad_out, index * group_rows, group_rows, 0)
        rows_attn = lax.dynamic_slice_in_dim(attn_out, index * group_rows, group_rows, 0)
        partial_sum = lax.dot_general(rows_out, rows_attn, (((0,), (0,)), ((), ())), preferred_element_type=jnp.float32)
        return (total + rounded(partial_sum).astype(jnp.float32), None)
    total, unused = lax.scan(add_group, jnp.zeros((D, width), jnp.float32), jnp.arange(N_COL, dtype=jnp.int32))
    grad_weight = total.astype(jnp.bfloat16)
    return (grad_q, grad_k, grad_v, grad_ck.reshape(CACHE, width), grad_cv.reshape(CACHE, width), grad_weight)
```

```python
import functools
import math

import jax
import jax.numpy as jnp
from jax import lax
from jax.experimental import pallas as pl
from jax.experimental.pallas import tpu as pltpu
from jax.sharding import PartitionSpec as P

HD=128; BLK=128; KB=4; CB=8
SCALE=1.0/math.sqrt(HD); EXPSCALE=SCALE*math.log2(math.e)
NT=(((1,),(1,)),((),())); TN=(((0,),(0,)),((),())); NN=(((1,),(0,)),((),()))
def dg(a,b,dims): return lax.dot_general(a,b,dims,preferred_element_type=jnp.float32)

def fwd_kernel(heads,table,q_ref,k_ref,v_ref,c_ref,o_ref,p_ref):
    b=pl.program_id(0); width=heads*HD
    keyp=lax.broadcasted_iota(jnp.int32,(BLK,BLK),0); qp=lax.broadcasted_iota(jnp.int32,(BLK,BLK),1)
    rows=[pl.ds(pl.multiple_of(table[b,j]*BLK,BLK),BLK) for j in range(KB)]
    for h in range(heads):
        cols=slice(h*HD,(h+1)*HD); vcols=slice(width+h*HD,width+(h+1)*HD)
        q=q_ref[:,cols]
        s=[dg(c_ref[r,cols],q,NT) for r in rows]
        s.append(jnp.where(keyp<=qp,dg(k_ref[:,cols],q,NT),-jnp.inf))
        m=functools.reduce(jnp.maximum,[jnp.max(t,axis=0,keepdims=True) for t in s])
        e=[jnp.exp2((t-m)*EXPSCALE) for t in s]
        l=functools.reduce(jnp.add,[jnp.sum(t,axis=0,keepdims=True) for t in e])
        r=1.0/l
        p=[(t*r).astype(jnp.bfloat16) for t in e]
        o=dg(p[KB],v_ref[:,cols],TN)
        for j in range(KB): o=o+dg(p[j],c_ref[rows[j],vcols],TN)
        o_ref[:,cols]=o.astype(jnp.bfloat16)
        for j in range(KB+1): p_ref[0,h,j*BLK:(j+1)*BLK,:]=p[j]

def fwd(table,q,k,v,cache):
    T,W=q.shape; heads=W//HD; nb=T//BLK
    blk=pl.BlockSpec((BLK,W),lambda b,t:(b,0))
    return pl.pallas_call(functools.partial(fwd_kernel,heads),
        grid_spec=pltpu.PrefetchScalarGridSpec(num_scalar_prefetch=1,grid=(nb,),
            in_specs=[blk,blk,blk,pl.BlockSpec(cache.shape,lambda b,t:(0,0))],
            out_specs=[blk,pl.BlockSpec((1,heads,(KB+1)*BLK,BLK),lambda b,t:(b,0,0,0))]),
        out_shape=[jax.ShapeDtypeStruct((T,W),jnp.bfloat16),jax.ShapeDtypeStruct((nb,heads,(KB+1)*BLK,BLK),jnp.bfloat16)],
        compiler_params=pltpu.CompilerParams(vmem_limit_bytes=40<<20),
        cost_estimate=pl.CostEstimate(flops=int(2*2*T*W*(KB+1)*BLK),bytes_accessed=12<<20,transcendentals=T*heads*(KB+1)*BLK),
        name="attn_fwd")(table,q,k,v,cache)

def bwd_kernel(heads,table,q_ref,k_ref,v_ref,c_ref,p_ref,ga_ref,gb_ref,dq_ref,dk_ref,dv_ref,dc_ref,acc):
    b=pl.program_id(0); width=heads*HD
    @pl.when(b==0)
    def _(): acc[...]=jnp.zeros_like(acc)
    rows=[pl.ds(pl.multiple_of(table[b,j]*BLK,BLK),BLK) for j in range(KB)]
    for h in range(heads):
        cols=slice(h*HD,(h+1)*HD); vcols=slice(width+h*HD,width+(h+1)*HD)
        q=q_ref[:,cols]
        do=(ga_ref[:,cols]+gb_ref[:,cols].astype(jnp.float32)).astype(jnp.bfloat16)
        kk=[c_ref[r,cols] for r in rows]+[k_ref[:,cols]]
        vv=[c_ref[r,vcols] for r in rows]+[v_ref[:,cols]]
        pb=[p_ref[0,h,j*BLK:(j+1)*BLK,:] for j in range(KB+1)]
        pf=[t.astype(jnp.float32) for t in pb]
        dp=[dg(t,do,NT) for t in vv]
        delta=functools.reduce(jnp.add,[jnp.sum(a*c,axis=0,keepdims=True) for a,c in zip(pf,dp)])
        ds=[(a*(c-delta)).astype(jnp.bfloat16) for a,c in zip(pf,dp)]
        dq=functools.reduce(jnp.add,[dg(a,c,TN) for a,c in zip(ds,kk)])
        dq_ref[:,cols]=(dq*SCALE).astype(jnp.bfloat16)
        dk_ref[:,cols]=(dg(ds[KB],q,NN)*SCALE).astype(jnp.bfloat16)
        dv_ref[:,cols]=dg(pb[KB],do,NN).astype(jnp.bfloat16)
        for j in range(KB):
            acc[rows[j],cols]+=dg(ds[j],q,NN)
            acc[rows[j],vcols]+=dg(pb[j],do,NN)
    @pl.when(b==pl.num_programs(0)-1)
    def _():
        dc_ref[:,:width]=(acc[:,:width]*SCALE).astype(jnp.bfloat16)
        dc_ref[:,width:]=acc[:,width:].astype(jnp.bfloat16)

def bwd(table,q,k,v,cache,p,ga,gb):
    T,W=q.shape; heads=W//HD; nb=T//BLK
    blk=pl.BlockSpec((BLK,W),lambda b,t:(b,0))
    full=pl.BlockSpec(cache.shape,lambda b,t:(0,0))
    return pl.pallas_call(functools.partial(bwd_kernel,heads),
        grid_spec=pltpu.PrefetchScalarGridSpec(num_scalar_prefetch=1,grid=(nb,),
            in_specs=[blk,blk,blk,full,pl.BlockSpec((1,heads,(KB+1)*BLK,BLK),lambda b,t:(b,0,0,0)),blk,blk],
            out_specs=[blk,blk,blk,full],
            scratch_shapes=[pltpu.VMEM(cache.shape,jnp.float32)]),
        out_shape=[jax.ShapeDtypeStruct((T,W),jnp.bfloat16)]*3+[jax.ShapeDtypeStruct(cache.shape,jnp.bfloat16)],
        compiler_params=pltpu.CompilerParams(vmem_limit_bytes=40<<20),
        cost_estimate=pl.CostEstimate(flops=int(4*2*T*W*(KB+1)*BLK),bytes_accessed=20<<20,transcendentals=0),
        name="attn_bwd")(table,q,k,v,cache,p,ga,gb)


AXES = ("row", "col")
PLACE = {0: 0, 3: 1, 1: 2, 2: 3}


def device(xh, y, z, xl, core):
    return (xh * 4 + y) * 16 + (z * 2 + xl) * 2 + core


def every():
    for xh in range(2):
        for y in range(4):
            for z in range(4):
                for xl in range(2):
                    for core in range(2):
                        yield xh, y, z, xl, core


def shifted(xh=0, y=0, z=0, xl=0, core=0):
    return [
        (device(*d), device(d[0] ^ xh, (d[1] + y) % 4, (d[2] + z) % 4, d[3] ^ xl, d[4] ^ core)) for d in every()
    ]


def swap_pairs():
    pairs = []
    for d in every():
        xh, y, z, xl, core = d
        owner = z // 2
        place = PLACE[((z % 2) * 2 + xl - y) % 4]
        pairs.append((device(*d), device(owner, y, (xh ^ owner) * 2 + place // 2, place % 2, core)))
    return pairs


def send(array, pairs):
    return lax.ppermute(array, AXES, pairs)


def f32(array):
    return array.astype(jnp.float32)


def per_device(grad_out, proj_weight, queries, keys, values, cache_keys, cache_values, block_table):
    bf16 = jnp.bfloat16
    tokens, width = queries.shape
    depth = grad_out.shape[1]
    swap = swap_pairs()
    back = [(b, a) for a, b in swap]
    col = lax.axis_index("col")
    z, xl = col // 4, (col // 2) % 2

    mine = jnp.concatenate([cache_keys, cache_values], axis=1)
    pair = jnp.concatenate([mine, send(mine, shifted(xl=1))], axis=0)
    own_core = jnp.concatenate(
        [pair, send(pair, shifted(z=1)), send(pair, shifted(z=3)), send(pair, shifted(z=2))], axis=0
    )
    other_core = send(own_core, shifted(core=1))
    rows = mine.shape[0]
    cache = jnp.stack(
        [own_core.reshape(CB, rows, 2 * width), other_core.reshape(CB, rows, 2 * width)], axis=1
    ).reshape(CB * 2 * rows, 2 * width)
    far = (block_table // 2 - z) % 4
    table = jnp.where(far == 0, 0, jnp.where(far == 3, 1, jnp.where(far == 1, 2, 3))) * 2 + ((block_table % 2) ^ xl)

    weight = lax.all_gather(send(proj_weight, swap), "col", axis=0, tiled=True)
    half = weight.shape[0] // 2

    before = send(grad_out, shifted(y=1))
    after = send(grad_out, shifted(y=3))
    across = jnp.concatenate(
        [send(before[: tokens // 2], shifted(y=1)), send(after[tokens // 2 :], shifted(y=3))], axis=0
    )
    columns = jnp.concatenate([grad_out, before, after, across], axis=1)

    attn_out, probs = fwd(table, queries, keys, values, cache)
    attn_other = send(attn_out, shifted(xh=1))

    other_part = jnp.dot(columns, weight[half:], preferred_element_type=jnp.float32).astype(bf16)
    from_other = send(other_part, shifted(xh=1))
    own_part = jnp.dot(columns, weight[:half], preferred_element_type=jnp.float32)

    def weight_part(attn):
        return lax.dot_general(
            columns, attn, (((0,), (0,)), ((), ())), preferred_element_type=jnp.float32
        ).astype(bf16)

    partial = jnp.concatenate([weight_part(attn_out), weight_part(attn_other)], axis=0)
    grad_weight = send(lax.psum_scatter(partial, "col", scatter_dimension=0, tiled=True), back)

    grad_q, grad_k, grad_v, grad_cache = bwd(table, queries, keys, values, cache, probs, own_part, from_other)

    parts = grad_cache.reshape(CB, 2, rows, 2 * width)
    total = (f32(parts[:, 0]) + f32(send(parts[:, 1], shifted(core=1)))).astype(bf16)
    total = total.reshape(4, 2, rows, 2 * width)
    total = (
        f32(total[0]) + f32(send(total[1], shifted(z=3))) + f32(send(total[2], shifted(z=1))) + f32(send(total[3], shifted(z=2)))
    ).astype(bf16)
    total = f32(total[0]) + f32(send(total[1], shifted(xl=1)))
    return (grad_q, grad_k, grad_v, total[:, :width], total[:, width:], grad_weight)


def solution(mesh):
    both = P("col", "row")
    return jax.shard_map(
        per_device, mesh=mesh, in_specs=(both,) * 7 + (P("col", None),), out_specs=(both,) * 6, check_vma=False
    )
```

```python
import functools
import math

import jax
import jax.numpy as jnp
import numpy as np
from jax import lax
from jax.experimental import pallas as pl
from jax.experimental.pallas import tpu as pltpu
from jax.sharding import PartitionSpec as P

HD=128; BLK=128; KB=4; CB=8
SCALE=1.0/math.sqrt(HD); EXPSCALE=SCALE*math.log2(math.e)
HALF, CHUNKS, CORE, SLOTS, KEPT = 0, 2, 10, 12, 16
STEPS = (0, 3, 1, 2)
NT=(((1,),(1,)),((),())); TN=(((0,),(0,)),((),())); NN=(((1,),(0,)),((),()))
def dg(a,b,dims): return lax.dot_general(a,b,dims,preferred_element_type=jnp.float32)

def fwd_kernel(heads,table,q_ref,k_ref,v_ref,c_ref,o_ref,p_ref):
    b=pl.program_id(0); width=heads*HD
    keyp=lax.broadcasted_iota(jnp.int32,(BLK,BLK),0); qp=lax.broadcasted_iota(jnp.int32,(BLK,BLK),1)
    rows=[pl.ds(pl.multiple_of(table[b,j]*BLK,BLK),BLK) for j in range(KB)]
    for h in range(heads):
        cols=slice(h*HD,(h+1)*HD); vcols=slice(width+h*HD,width+(h+1)*HD)
        q=q_ref[:,cols]
        s=[dg(c_ref[r,cols],q,NT) for r in rows]
        s.append(jnp.where(keyp<=qp,dg(k_ref[:,cols],q,NT),-jnp.inf))
        m=functools.reduce(jnp.maximum,[jnp.max(t,axis=0,keepdims=True) for t in s])
        e=[jnp.exp2((t-m)*EXPSCALE) for t in s]
        l=functools.reduce(jnp.add,[jnp.sum(t,axis=0,keepdims=True) for t in e])
        r=1.0/l
        p=[(t*r).astype(jnp.bfloat16) for t in e]
        o=dg(p[KB],v_ref[:,cols],TN)
        for j in range(KB): o=o+dg(p[j],c_ref[rows[j],vcols],TN)
        o_ref[:,cols]=o.astype(jnp.bfloat16)
        for j in range(KB+1): p_ref[0,h,j*BLK:(j+1)*BLK,:]=p[j]

def fwd(table,q,k,v,cache):
    T,W=q.shape; heads=W//HD; nb=T//BLK
    blk=pl.BlockSpec((BLK,W),lambda b,t:(b,0))
    return pl.pallas_call(functools.partial(fwd_kernel,heads),
        grid_spec=pltpu.PrefetchScalarGridSpec(num_scalar_prefetch=1,grid=(nb,),
            in_specs=[blk,blk,blk,pl.BlockSpec(cache.shape,lambda b,t:(0,0))],
            out_specs=[blk,pl.BlockSpec((1,heads,(KB+1)*BLK,BLK),lambda b,t:(b,0,0,0))]),
        out_shape=[jax.ShapeDtypeStruct((T,W),jnp.bfloat16),jax.ShapeDtypeStruct((nb,heads,(KB+1)*BLK,BLK),jnp.bfloat16)],
        compiler_params=pltpu.CompilerParams(vmem_limit_bytes=40<<20),
        cost_estimate=pl.CostEstimate(flops=int(2*2*T*W*(KB+1)*BLK),bytes_accessed=12<<20,transcendentals=T*heads*(KB+1)*BLK),
        name="attn_fwd")(table,q,k,v,cache)

def bwd_kernel(heads,table,place,q_ref,k_ref,v_ref,c_ref,p_ref,ga_ref,gb_ref,dq_ref,dk_ref,dv_ref,keep_ref,away_ref,acc):
    b=pl.program_id(0); width=heads*HD
    @pl.when(b==0)
    def _(): acc[...]=jnp.zeros_like(acc)
    rows=[pl.ds(pl.multiple_of(table[b,j]*BLK,BLK),BLK) for j in range(KB)]
    kept=[pl.ds(pl.multiple_of(place[KEPT+table[b,j]]*BLK,BLK),BLK) for j in range(KB)]
    for h in range(heads):
        cols=slice(h*HD,(h+1)*HD); vcols=slice(width+h*HD,width+(h+1)*HD)
        q=q_ref[:,cols]
        do=(ga_ref[:,cols]+gb_ref[:,cols].astype(jnp.float32)).astype(jnp.bfloat16)
        kk=[c_ref[r,cols] for r in rows]+[k_ref[:,cols]]
        vv=[c_ref[r,vcols] for r in rows]+[v_ref[:,cols]]
        pb=[p_ref[0,h,j*BLK:(j+1)*BLK,:] for j in range(KB+1)]
        pf=[t.astype(jnp.float32) for t in pb]
        dp=[dg(t,do,NT) for t in vv]
        delta=functools.reduce(jnp.add,[jnp.sum(a*c,axis=0,keepdims=True) for a,c in zip(pf,dp)])
        ds=[(a*(c-delta)).astype(jnp.bfloat16) for a,c in zip(pf,dp)]
        dq=functools.reduce(jnp.add,[dg(a,c,TN) for a,c in zip(ds,kk)])
        dq_ref[:,cols]=(dq*SCALE).astype(jnp.bfloat16)
        dk_ref[:,cols]=(dg(ds[KB],q,NN)*SCALE).astype(jnp.bfloat16)
        dv_ref[:,cols]=dg(pb[KB],do,NN).astype(jnp.bfloat16)
        for j in range(KB):
            acc[kept[j],cols]+=dg(ds[j],q,NN)
            acc[kept[j],vcols]+=dg(pb[j],do,NN)
    @pl.when(b==pl.num_programs(0)-1)
    def _():
        half=BLK//2
        for ref,core in ((keep_ref,place[CORE]),(away_ref,place[CORE+1])):
            for c in range(CB):
                at=pl.ds(pl.multiple_of(c*BLK+core*half,half),half)
                ref[c*half:(c+1)*half,:width]=(acc[at,:width]*SCALE).astype(jnp.bfloat16)
                ref[c*half:(c+1)*half,width:]=acc[at,width:].astype(jnp.bfloat16)

def bwd(table,place,q,k,v,cache,p,ga,gb):
    T,W=q.shape; heads=W//HD; nb=T//BLK
    blk=pl.BlockSpec((BLK,W),lambda b,t,w:(b,0))
    full=pl.BlockSpec(cache.shape,lambda b,t,w:(0,0))
    part=pl.BlockSpec((cache.shape[0]//2,cache.shape[1]),lambda b,t,w:(0,0))
    return pl.pallas_call(functools.partial(bwd_kernel,heads),
        grid_spec=pltpu.PrefetchScalarGridSpec(num_scalar_prefetch=2,grid=(nb,),
            in_specs=[blk,blk,blk,full,pl.BlockSpec((1,heads,(KB+1)*BLK,BLK),lambda b,t,w:(b,0,0,0)),blk,blk],
            out_specs=[blk,blk,blk,part,part],
            scratch_shapes=[pltpu.VMEM(cache.shape,jnp.float32)]),
        out_shape=[jax.ShapeDtypeStruct((T,W),jnp.bfloat16)]*3+[jax.ShapeDtypeStruct((cache.shape[0]//2,cache.shape[1]),jnp.bfloat16)]*2,
        compiler_params=pltpu.CompilerParams(vmem_limit_bytes=40<<20),
        cost_estimate=pl.CostEstimate(flops=int(4*2*T*W*(KB+1)*BLK),bytes_accessed=20<<20,transcendentals=0),
        name="attn_bwd")(table,place,q,k,v,cache,p,ga,gb)


VMEM_LIMIT = 56 << 20


def project_kernel(other, place, *refs):
    w_ref, o_ref = refs[-2:]
    depth = refs[0].shape[1]

    def total(half):
        parts = []
        for j in range(4):
            rows = pl.ds(pl.multiple_of(place[CHUNKS + 4 * other + j] * depth, depth), depth)
            parts.append(dg(refs[2 * j + half][...], w_ref[rows, :], NN))
        return functools.reduce(jnp.add, parts).astype(o_ref.dtype)

    first = pl.program_id(0) < pl.num_programs(0) // 2

    @pl.when(first)
    def _():
        o_ref[...] = total(0)

    @pl.when(jnp.logical_not(first))
    def _():
        o_ref[...] = total(1)


def project(other, place, columns, weight, dtype):
    half, depth = columns[0].shape
    width = weight.shape[1]
    steps = 4
    block = 2 * half // steps
    upper = pl.BlockSpec((block, depth), lambda i, p: (jnp.minimum(i, steps // 2 - 1), 0))
    lower = pl.BlockSpec((block, depth), lambda i, p: (jnp.maximum(i - steps // 2, 0), 0))
    return pl.pallas_call(
        functools.partial(project_kernel, other),
        grid_spec=pltpu.PrefetchScalarGridSpec(
            num_scalar_prefetch=1,
            grid=(steps,),
            in_specs=[upper, lower] * 4 + [pl.BlockSpec((4 * depth, width), lambda i, p: (p[HALF + other], 0))],
            out_specs=pl.BlockSpec((block, width), lambda i, p: (i, 0)),
        ),
        out_shape=jax.ShapeDtypeStruct((2 * half, width), dtype),
        compiler_params=pltpu.CompilerParams(vmem_limit_bytes=VMEM_LIMIT),
        cost_estimate=pl.CostEstimate(flops=16 * half * depth * width, bytes_accessed=14 << 20, transcendentals=0),
        name="project",
    )(place, *columns, weight)


def outer_kernel(place, *refs):
    chunks, own, other, rest = refs[:8], refs[8], refs[9], refs[10:]
    picked, attn = rest[-2:]
    half = chunks[0].shape[0]
    width = own.shape[1]
    upper = place[HALF]

    @pl.when(upper == 0)
    def _():
        attn[:, :width] = own[...]
        attn[:, width:] = other[...]

    @pl.when(upper != 0)
    def _():
        attn[:, :width] = other[...]
        attn[:, width:] = own[...]

    for slot in range(4):
        for j in range(4):

            @pl.when(place[SLOTS + slot] == j)
            def _():
                picked[:half, :] = chunks[2 * j][...]
                picked[half:, :] = chunks[2 * j + 1][...]

        out = dg(picked[...], attn[...], TN)
        size = out.shape[0]
        here = slice(slot * size, (slot + 1) * size)
        if len(rest) == 3:
            rest[0][here, :] = out.astype(jnp.bfloat16)
        else:
            out = (out + rest[0][here, :].astype(jnp.float32)).astype(jnp.bfloat16)
            for f in range(2):
                away = f + upper - 2 * f * upper
                to = 4 * f + slot + away * (3 - 2 * slot)
                rest[1][pl.ds(pl.multiple_of(to * size, size), size), :] = out[:, f * width : (f + 1) * width]


def outer(place, columns, own, other, added=None):
    half, depth = columns[0].shape
    width = own.shape[1]
    size = depth // 2
    core = CORE + int(added is None)
    full = pl.BlockSpec(own.shape, lambda i, p: (0, 0))
    both = pl.BlockSpec((4 * size, 2 * width), lambda i, p: (0, 0))
    shape = (4 * size, 2 * width) if added is None else (8 * size, width)
    return pl.pallas_call(
        outer_kernel,
        grid_spec=pltpu.PrefetchScalarGridSpec(
            num_scalar_prefetch=1,
            grid=(1,),
            in_specs=[pl.BlockSpec((half, size), lambda i, p: (0, p[core]))] * 8
            + [full, full]
            + ([] if added is None else [both]),
            out_specs=pl.BlockSpec(shape, lambda i, p: (0, 0)),
            scratch_shapes=[pltpu.VMEM((2 * half, size), jnp.bfloat16), pltpu.VMEM((2 * half, 2 * width), jnp.bfloat16)],
        ),
        out_shape=jax.ShapeDtypeStruct(shape, jnp.bfloat16),
        compiler_params=pltpu.CompilerParams(vmem_limit_bytes=VMEM_LIMIT),
        cost_estimate=pl.CostEstimate(flops=32 * half * size * width, bytes_accessed=12 << 20, transcendentals=0),
        name="outer",
    )(place, *columns, own, other, *([] if added is None else [added]))


AXES = ("row", "col")

def device(xh, y, z, xl, core):
    return (xh * 4 + y) * 16 + (z * 2 + xl) * 2 + core


def every():
    for xh in range(2):
        for y in range(4):
            for z in range(4):
                for xl in range(2):
                    for core in range(2):
                        yield xh, y, z, xl, core


def shifted(xh=0, y=0, z=0, xl=0, core=0):
    return [
        (device(*d), device(d[0] ^ xh, (d[1] + y) % 4, (d[2] + z) % 4, d[3] ^ xl, d[4] ^ core)) for d in every()
    ]


def swap_pairs():
    pairs = []
    for d in every():
        xh, y, z, xl, core = d
        upper, lower = z // 2, z % 2
        away = int(upper != xh)
        pairs.append((device(*d), device(upper, y, xh * 2 + (lower ^ away), xl ^ away, core)))
    return pairs


def place_table():
    rows = []
    for xh, y, z, xl, core in every():
        owners = [(y + step) % 4 for step in STEPS]
        rows.append(
            [xh, 1 - xh, *owners, *(3 - o for o in owners), core, 1 - core, *(owners.index(t) for t in range(4))]
            + [STEPS.index((c // 2 - z) % 4) * 2 + (c % 2 ^ xl) for c in range(CB)]
        )
    return np.array(rows, np.int32)


def send(array, pairs):
    return lax.ppermute(array, AXES, pairs)


def f32(array):
    return array.astype(jnp.float32)


def per_device(grad_out, proj_weight, queries, keys, values, cache_keys, cache_values, block_table):
    bf16 = jnp.bfloat16
    tokens, width = queries.shape
    depth = grad_out.shape[1]
    place = lax.dynamic_index_in_dim(
        jnp.asarray(place_table()), lax.axis_index("row") * 16 + lax.axis_index("col"), keepdims=False
    )
    swap = swap_pairs()
    half = tokens // 2

    rows = cache_keys.shape[0]
    mine = jnp.concatenate([cache_keys, cache_values], axis=1)
    cache = lax.all_gather(mine, "col", axis=0, tiled=True)

    upper, lower = grad_out[:half], grad_out[half:]
    before_upper, after_lower = send(upper, shifted(y=1)), send(lower, shifted(y=3))
    before_lower, after_upper = send(lower, shifted(y=1)), send(upper, shifted(y=3))
    swapped, before_upper, after_lower = lax.optimization_barrier((send(proj_weight, swap), before_upper, after_lower))
    weight = lax.all_gather(swapped, "col", axis=0, tiled=True)
    columns = (
        upper,
        lower,
        before_upper,
        before_lower,
        after_upper,
        after_lower,
        send(before_upper, shifted(y=1)),
        send(after_lower, shifted(y=3)),
    )

    attn_out, probs = fwd(block_table, queries, keys, values, cache)
    attn_other = send(attn_out, shifted(xh=1))

    theirs = outer(place, columns, attn_out, attn_other)
    theirs, other_part = lax.optimization_barrier((theirs, project(1, place, columns, weight, bf16)))
    from_other = send(other_part, shifted(xh=1))
    own_part = project(0, place, columns, weight, jnp.float32)
    pieces = outer(place, columns, attn_out, attn_other, send(theirs, shifted(core=1)))
    pieces, from_other, own_part = lax.optimization_barrier((pieces, from_other, own_part))
    groups = [[2 * i + c for i in range(8)] for c in range(2)]
    pieces = lax.all_to_all(pieces, "col", split_axis=0, concat_axis=0, axis_index_groups=groups, tiled=True)
    total = jnp.sum(f32(pieces.reshape(8, -1, width)), axis=0).astype(bf16)
    grad_weight = send(total, swap)

    grad_q, grad_k, grad_v, keep, away = bwd(
        block_table, place, queries, keys, values, cache, probs, own_part, from_other
    )
    parts = (f32(keep) + f32(send(away, shifted(core=1)))).astype(bf16).reshape(4, 2 * rows, 2 * width)
    parts = sum([f32(parts[0])] + [f32(send(parts[i], shifted(z=STEPS[i]))) for i in range(1, 4)]).astype(bf16)
    total = f32(parts[:rows]) + f32(send(parts[rows:], shifted(xl=1)))
    return (grad_q, grad_k, grad_v, total[:, :width], total[:, width:], grad_weight)


def solution(mesh):
    both = P("col", "row")
    return jax.shard_map(
        per_device, mesh=mesh, in_specs=(both,) * 7 + (P("col", None),), out_specs=(both,) * 6, check_vma=False
    )
```

```python
import functools
import math

import jax
import jax.numpy as jnp
import numpy as np
from jax import lax
from jax.experimental import pallas as pl
from jax.experimental.pallas import tpu as pltpu
from jax.sharding import PartitionSpec as P

HD=128; BLK=128; KB=4; CB=8
SCALE=1.0/math.sqrt(HD); EXPSCALE=SCALE*math.log2(math.e)
SHORT = pl.CostEstimate(flops=1 << 20, bytes_accessed=1 << 16, transcendentals=0)
HALF, CHUNKS, CORE, SLOTS, KEPT = 0, 2, 10, 12, 16
STEPS = (0, 3, 1, 2)
NT=(((1,),(1,)),((),())); TN=(((0,),(0,)),((),())); NN=(((1,),(0,)),((),()))
def dg(a,b,dims): return lax.dot_general(a,b,dims,preferred_element_type=jnp.float32)

def fwd_kernel(heads,table,place,q_ref,k_ref,v_ref,c_ref,o_ref,p_ref):
    b=pl.program_id(0); width=heads*HD
    keyp=lax.broadcasted_iota(jnp.int32,(BLK,BLK),0); qp=lax.broadcasted_iota(jnp.int32,(BLK,BLK),1)
    rows=[pl.ds(pl.multiple_of(place[KEPT+table[b,j]]*BLK,BLK),BLK) for j in range(KB)]
    for h in range(heads):
        cols=slice(h*HD,(h+1)*HD); vcols=slice(width+h*HD,width+(h+1)*HD)
        q=q_ref[:,cols]
        s=[dg(c_ref[r,cols],q,NT) for r in rows]
        s.append(jnp.where(keyp<=qp,dg(k_ref[:,cols],q,NT),-jnp.inf))
        m=functools.reduce(jnp.maximum,[jnp.max(t,axis=0,keepdims=True) for t in s])
        e=[jnp.exp2((t-m)*EXPSCALE) for t in s]
        l=functools.reduce(jnp.add,[jnp.sum(t,axis=0,keepdims=True) for t in e])
        r=1.0/l
        p=[(t*r).astype(jnp.bfloat16) for t in e]
        o=dg(p[KB],v_ref[:,cols],TN)
        for j in range(KB): o=o+dg(p[j],c_ref[rows[j],vcols],TN)
        o_ref[:,cols]=o.astype(jnp.bfloat16)
        for j in range(KB+1): p_ref[0,h,j*BLK:(j+1)*BLK,:]=p[j]

def fwd(table,place,q,k,v,cache):
    T,W=q.shape; heads=W//HD; nb=T//BLK
    blk=pl.BlockSpec((BLK,W),lambda b,t,w:(b,0))
    return pl.pallas_call(functools.partial(fwd_kernel,heads),
        grid_spec=pltpu.PrefetchScalarGridSpec(num_scalar_prefetch=2,grid=(nb,),
            in_specs=[blk,blk,blk,pl.BlockSpec(cache.shape,lambda b,t,w:(0,0))],
            out_specs=[blk,pl.BlockSpec((1,heads,(KB+1)*BLK,BLK),lambda b,t,w:(b,0,0,0))]),
        out_shape=[jax.ShapeDtypeStruct((T,W),jnp.bfloat16),jax.ShapeDtypeStruct((nb,heads,(KB+1)*BLK,BLK),jnp.bfloat16)],
        compiler_params=pltpu.CompilerParams(vmem_limit_bytes=40<<20),
        cost_estimate=SHORT,
        name="attn_fwd")(table,place,q,k,v,cache)

def bwd_kernel(heads,table,place,q_ref,k_ref,v_ref,c_ref,p_ref,ga_ref,gb_ref,dq_ref,dk_ref,dv_ref,keep_ref,away_ref,acc):
    b=pl.program_id(0); width=heads*HD
    @pl.when(b==0)
    def _(): acc[...]=jnp.zeros_like(acc)
    rows=[pl.ds(pl.multiple_of(place[KEPT+table[b,j]]*BLK,BLK),BLK) for j in range(KB)]
    for h in range(heads):
        cols=slice(h*HD,(h+1)*HD); vcols=slice(width+h*HD,width+(h+1)*HD)
        q=q_ref[:,cols]
        do=(ga_ref[:,cols]+gb_ref[:,cols].astype(jnp.float32)).astype(jnp.bfloat16)
        kk=[c_ref[r,cols] for r in rows]+[k_ref[:,cols]]
        vv=[c_ref[r,vcols] for r in rows]+[v_ref[:,cols]]
        pb=[p_ref[0,h,j*BLK:(j+1)*BLK,:] for j in range(KB+1)]
        pf=[t.astype(jnp.float32) for t in pb]
        dp=[dg(t,do,NT) for t in vv]
        delta=functools.reduce(jnp.add,[jnp.sum(a*c,axis=0,keepdims=True) for a,c in zip(pf,dp)])
        ds=[(a*(c-delta)).astype(jnp.bfloat16) for a,c in zip(pf,dp)]
        dq=functools.reduce(jnp.add,[dg(a,c,TN) for a,c in zip(ds,kk)])
        dq_ref[:,cols]=(dq*SCALE).astype(jnp.bfloat16)
        dk_ref[:,cols]=(dg(ds[KB],q,NN)*SCALE).astype(jnp.bfloat16)
        dv_ref[:,cols]=dg(pb[KB],do,NN).astype(jnp.bfloat16)
        for j in range(KB):
            acc[rows[j],cols]+=dg(ds[j],q,NN)
            acc[rows[j],vcols]+=dg(pb[j],do,NN)
    @pl.when(b==pl.num_programs(0)-1)
    def _():
        half=BLK//2
        for i,ref in enumerate((keep_ref,away_ref)):
            for c in range(CB):
                at=slice(c*BLK+i*half,c*BLK+(i+1)*half)
                ref[c*half:(c+1)*half,:width]=(acc[at,:width]*SCALE).astype(jnp.bfloat16)
                ref[c*half:(c+1)*half,width:]=acc[at,width:].astype(jnp.bfloat16)

def bwd(table,place,q,k,v,cache,p,ga,gb):
    T,W=q.shape; heads=W//HD; nb=T//BLK
    blk=pl.BlockSpec((BLK,W),lambda b,t,w:(b,0))
    full=pl.BlockSpec(cache.shape,lambda b,t,w:(0,0))
    part=pl.BlockSpec((cache.shape[0]//2,cache.shape[1]),lambda b,t,w:(0,0))
    return pl.pallas_call(functools.partial(bwd_kernel,heads),
        grid_spec=pltpu.PrefetchScalarGridSpec(num_scalar_prefetch=2,grid=(nb,),
            in_specs=[blk,blk,blk,full,pl.BlockSpec((1,heads,(KB+1)*BLK,BLK),lambda b,t,w:(b,0,0,0)),blk,blk],
            out_specs=[blk,blk,blk,part,part],
            scratch_shapes=[pltpu.VMEM(cache.shape,jnp.float32)]),
        out_shape=[jax.ShapeDtypeStruct((T,W),jnp.bfloat16)]*3+[jax.ShapeDtypeStruct((cache.shape[0]//2,cache.shape[1]),jnp.bfloat16)]*2,
        compiler_params=pltpu.CompilerParams(vmem_limit_bytes=40<<20),
        cost_estimate=SHORT,
        name="attn_bwd")(table,place,q,k,v,cache,p,ga,gb)


VMEM_LIMIT = 56 << 20


def project_kernel(other, place, *refs):
    w_ref, o_ref = refs[-2:]
    depth = refs[0].shape[1]

    def total(half):
        parts = []
        for j in range(4):
            rows = pl.ds(pl.multiple_of(place[CHUNKS + 4 * other + j] * depth, depth), depth)
            parts.append(dg(refs[2 * j + half][...], w_ref[rows, :], NN))
        return functools.reduce(jnp.add, parts).astype(o_ref.dtype)

    first = pl.program_id(0) < pl.num_programs(0) // 2

    @pl.when(first)
    def _():
        o_ref[...] = total(0)

    @pl.when(jnp.logical_not(first))
    def _():
        o_ref[...] = total(1)


def project(other, place, columns, weight, dtype):
    half, depth = columns[0].shape
    width = weight.shape[1]
    steps = 4
    block = 2 * half // steps
    upper = pl.BlockSpec((block, depth), lambda i, p: (jnp.minimum(i, steps // 2 - 1), 0))
    lower = pl.BlockSpec((block, depth), lambda i, p: (jnp.maximum(i - steps // 2, 0), 0))
    return pl.pallas_call(
        functools.partial(project_kernel, other),
        grid_spec=pltpu.PrefetchScalarGridSpec(
            num_scalar_prefetch=1,
            grid=(steps,),
            in_specs=[upper, lower] * 4 + [pl.BlockSpec((4 * depth, width), lambda i, p: (p[HALF + other], 0))],
            out_specs=pl.BlockSpec((block, width), lambda i, p: (i, 0)),
        ),
        out_shape=jax.ShapeDtypeStruct((2 * half, width), dtype),
        compiler_params=pltpu.CompilerParams(vmem_limit_bytes=VMEM_LIMIT),
        cost_estimate=SHORT,
        name="project",
    )(place, *columns, weight)


def outer_kernel(place, *refs):
    chunks, own, other, rest = refs[:8], refs[8], refs[9], refs[10:]
    picked, attn = rest[-2:]
    half = chunks[0].shape[0]
    width = own.shape[1]
    upper = place[HALF]

    @pl.when(upper == 0)
    def _():
        attn[:, :width] = own[...]
        attn[:, width:] = other[...]

    @pl.when(upper != 0)
    def _():
        attn[:, :width] = other[...]
        attn[:, width:] = own[...]

    for slot in range(4):
        for j in range(4):

            @pl.when(place[SLOTS + slot] == j)
            def _():
                picked[:half, :] = chunks[2 * j][...]
                picked[half:, :] = chunks[2 * j + 1][...]

        out = dg(picked[...], attn[...], TN)
        size = out.shape[0]
        here = slice(slot * size, (slot + 1) * size)
        if len(rest) == 3:
            rest[0][here, :] = out.astype(jnp.bfloat16)
        else:
            out = (out + rest[0][here, :].astype(jnp.float32)).astype(jnp.bfloat16)
            for f in range(2):
                away = f + upper - 2 * f * upper
                to = 4 * f + slot + away * (3 - 2 * slot)
                rest[1][pl.ds(pl.multiple_of(to * size, size), size), :] = out[:, f * width : (f + 1) * width]


def outer(place, columns, own, other, added=None):
    half, depth = columns[0].shape
    width = own.shape[1]
    size = depth // 2
    core = CORE + int(added is None)
    full = pl.BlockSpec(own.shape, lambda i, p: (0, 0))
    both = pl.BlockSpec((4 * size, 2 * width), lambda i, p: (0, 0))
    shape = (4 * size, 2 * width) if added is None else (8 * size, width)
    return pl.pallas_call(
        outer_kernel,
        grid_spec=pltpu.PrefetchScalarGridSpec(
            num_scalar_prefetch=1,
            grid=(1,),
            in_specs=[pl.BlockSpec((half, size), lambda i, p: (0, p[core]))] * 8
            + [full, full]
            + ([] if added is None else [both]),
            out_specs=pl.BlockSpec(shape, lambda i, p: (0, 0)),
            scratch_shapes=[pltpu.VMEM((2 * half, size), jnp.bfloat16), pltpu.VMEM((2 * half, 2 * width), jnp.bfloat16)],
        ),
        out_shape=jax.ShapeDtypeStruct(shape, jnp.bfloat16),
        compiler_params=pltpu.CompilerParams(vmem_limit_bytes=VMEM_LIMIT),
        cost_estimate=SHORT,
        name="outer",
    )(place, *columns, own, other, *([] if added is None else [added]))


AXES = ("row", "col")

def device(xh, y, z, xl, core):
    return (xh * 4 + y) * 16 + (z * 2 + xl) * 2 + core


def every():
    for xh in range(2):
        for y in range(4):
            for z in range(4):
                for xl in range(2):
                    for core in range(2):
                        yield xh, y, z, xl, core


def shifted(xh=0, y=0, z=0, xl=0, core=0):
    return [
        (device(*d), device(d[0] ^ xh, (d[1] + y) % 4, (d[2] + z) % 4, d[3] ^ xl, d[4] ^ core)) for d in every()
    ]


def swap_pairs():
    pairs = []
    for d in every():
        xh, y, z, xl, core = d
        upper, lower = z // 2, z % 2
        away = int(upper != xh)
        pairs.append((device(*d), device(upper, y, xh * 2 + (lower ^ away), xl ^ away, core)))
    return pairs


def place_table():
    rows = []
    for xh, y, z, xl, core in every():
        owners = [(y + step) % 4 for step in STEPS]
        rows.append(
            [xh, 1 - xh, *owners, *(3 - o for o in owners), core, 1 - core, *(owners.index(t) for t in range(4))]
            + [STEPS.index((c // 2 - z) % 4) * 2 + (c % 2 ^ xl) for c in range(CB)]
        )
    return np.array(rows, np.int32)


def send(array, pairs):
    return lax.ppermute(array, AXES, pairs)


def f32(array):
    return array.astype(jnp.float32)


def per_device(grad_out, proj_weight, queries, keys, values, cache_keys, cache_values, block_table):
    bf16 = jnp.bfloat16
    tokens, width = queries.shape
    depth = grad_out.shape[1]
    place = lax.dynamic_index_in_dim(
        jnp.asarray(place_table()), lax.axis_index("row") * 16 + lax.axis_index("col"), keepdims=False
    )
    swap = swap_pairs()
    half = tokens // 2

    rows = cache_keys.shape[0]
    mine = jnp.concatenate([cache_keys, cache_values], axis=1)
    pair = jnp.concatenate([mine, send(mine, shifted(xl=1))], axis=0)

    upper, lower = grad_out[:half], grad_out[half:]
    before_upper, after_lower = send(upper, shifted(y=1)), send(lower, shifted(y=3))
    before_lower, after_upper = send(lower, shifted(y=1)), send(upper, shifted(y=3))
    swapped, before_upper, after_lower, pair = lax.optimization_barrier(
        (send(proj_weight, swap), before_upper, after_lower, pair)
    )
    near = jnp.concatenate([pair] + [send(pair, shifted(z=4 - STEPS[i])) for i in range(1, 4)], axis=0)
    near, before_lower, after_upper = lax.optimization_barrier((near, before_lower, after_upper))
    far = send(near, shifted(core=1))
    cache = jnp.stack(
        [near.reshape(CB, rows, 2 * width), far.reshape(CB, rows, 2 * width)], axis=1
    ).reshape(2 * CB * rows, 2 * width)
    weight = lax.all_gather(swapped, "col", axis=0, tiled=True)
    columns = (
        upper,
        lower,
        before_upper,
        before_lower,
        after_upper,
        after_lower,
        send(before_upper, shifted(y=1)),
        send(after_lower, shifted(y=3)),
    )

    attn_out, probs = fwd(block_table, place, queries, keys, values, cache)
    attn_other = send(attn_out, shifted(xh=1))

    other_part, weight = lax.optimization_barrier((project(1, place, columns, weight, bf16), weight))
    own_part = project(0, place, columns, weight, jnp.float32)
    attn_other, own_part = lax.optimization_barrier((attn_other, own_part))
    theirs = outer(place, columns, attn_out, attn_other)
    from_other = send(other_part, shifted(xh=1))
    pieces = outer(place, columns, attn_out, attn_other, send(theirs, shifted(core=1)))
    pieces, from_other, own_part = lax.optimization_barrier((pieces, from_other, own_part))
    groups = [[2 * i + c for i in range(8)] for c in range(2)]
    pieces = lax.all_to_all(pieces, "col", split_axis=0, concat_axis=0, axis_index_groups=groups, tiled=True)
    total = jnp.sum(f32(pieces.reshape(8, -1, width)), axis=0).astype(bf16)
    grad_weight = send(total, swap)

    grad_q, grad_k, grad_v, keep, away = bwd(
        block_table, place, queries, keys, values, cache, probs, own_part, from_other
    )
    parts = (f32(keep) + f32(send(away, shifted(core=1)))).astype(bf16).reshape(4, 2 * rows, 2 * width)
    parts = sum([f32(parts[0])] + [f32(send(parts[i], shifted(z=STEPS[i]))) for i in range(1, 4)]).astype(bf16)
    total = f32(parts[:rows]) + f32(send(parts[rows:], shifted(xl=1)))
    return (grad_q, grad_k, grad_v, total[:, :width], total[:, width:], grad_weight)


def solution(mesh):
    both = P("col", "row")
    return jax.shard_map(
        per_device, mesh=mesh, in_specs=(both,) * 7 + (P("col", None),), out_specs=(both,) * 6, check_vma=False
    )
```

```python
import functools
import math

import jax
import jax.numpy as jnp
import numpy as np
from jax import lax
from jax.experimental import pallas as pl
from jax.experimental.pallas import tpu as pltpu
from jax.sharding import PartitionSpec as P

HD=128; BLK=128; KB=4; CB=8
SCALE=1.0/math.sqrt(HD); EXPSCALE=SCALE*math.log2(math.e)
SHORT = pl.CostEstimate(flops=1 << 20, bytes_accessed=1 << 16, transcendentals=0)
HALF, CHUNKS, CORE, SLOTS, KEPT = 0, 2, 10, 12, 16
STEPS = (0, 3, 1, 2)
NT=(((1,),(1,)),((),())); TN=(((0,),(0,)),((),())); NN=(((1,),(0,)),((),()))
def dg(a,b,dims): return lax.dot_general(a,b,dims,preferred_element_type=jnp.float32)

def fwd_kernel(heads,table,place,q_ref,k_ref,v_ref,c_ref,o_ref,p_ref):
    b=pl.program_id(0); width=heads*HD
    keyp=lax.broadcasted_iota(jnp.int32,(BLK,BLK),0); qp=lax.broadcasted_iota(jnp.int32,(BLK,BLK),1)
    rows=[pl.ds(pl.multiple_of(place[KEPT+table[b,j]]*BLK,BLK),BLK) for j in range(KB)]
    for h in range(heads):
        cols=slice(h*HD,(h+1)*HD); vcols=slice(width+h*HD,width+(h+1)*HD)
        q=q_ref[:,cols]
        s=[dg(c_ref[r,cols],q,NT) for r in rows]
        s.append(jnp.where(keyp<=qp,dg(k_ref[:,cols],q,NT),-jnp.inf))
        m=functools.reduce(jnp.maximum,[jnp.max(t,axis=0,keepdims=True) for t in s])
        e=[jnp.exp2((t-m)*EXPSCALE) for t in s]
        l=functools.reduce(jnp.add,[jnp.sum(t,axis=0,keepdims=True) for t in e])
        r=1.0/l
        p=[(t*r).astype(jnp.bfloat16) for t in e]
        o=dg(p[KB],v_ref[:,cols],TN)
        for j in range(KB): o=o+dg(p[j],c_ref[rows[j],vcols],TN)
        o_ref[:,cols]=o.astype(jnp.bfloat16)
        for j in range(KB+1): p_ref[0,h,j*BLK:(j+1)*BLK,:]=p[j]

def fwd(table,place,q,k,v,cache):
    T,W=q.shape; heads=W//HD; nb=T//BLK
    blk=pl.BlockSpec((BLK,W),lambda b,t,w:(b,0))
    return pl.pallas_call(functools.partial(fwd_kernel,heads),
        grid_spec=pltpu.PrefetchScalarGridSpec(num_scalar_prefetch=2,grid=(nb,),
            in_specs=[blk,blk,blk,pl.BlockSpec(cache.shape,lambda b,t,w:(0,0))],
            out_specs=[blk,pl.BlockSpec((1,heads,(KB+1)*BLK,BLK),lambda b,t,w:(b,0,0,0))]),
        out_shape=[jax.ShapeDtypeStruct((T,W),jnp.bfloat16),jax.ShapeDtypeStruct((nb,heads,(KB+1)*BLK,BLK),jnp.bfloat16)],
        compiler_params=pltpu.CompilerParams(vmem_limit_bytes=40<<20),
        cost_estimate=SHORT,
        name="attn_fwd")(table,place,q,k,v,cache)

def bwd_kernel(heads,table,place,q_ref,k_ref,v_ref,c_ref,p_ref,ga_ref,gu_ref,gl_ref,dq_ref,dk_ref,dv_ref,keep_ref,away_ref,acc):
    b=pl.program_id(0); width=heads*HD
    @pl.when(b==0)
    def _(): acc[...]=jnp.zeros_like(acc)
    rows=[pl.ds(pl.multiple_of(place[KEPT+table[b,j]]*BLK,BLK),BLK) for j in range(KB)]
    for h in range(heads):
        cols=slice(h*HD,(h+1)*HD); vcols=slice(width+h*HD,width+(h+1)*HD)
        q=q_ref[:,cols]
        gb=jnp.where(b<pl.num_programs(0)//2,gu_ref[:,cols].astype(jnp.float32),gl_ref[:,cols].astype(jnp.float32))
        do=(ga_ref[:,cols]+gb).astype(jnp.bfloat16)
        kk=[c_ref[r,cols] for r in rows]+[k_ref[:,cols]]
        vv=[c_ref[r,vcols] for r in rows]+[v_ref[:,cols]]
        pb=[p_ref[0,h,j*BLK:(j+1)*BLK,:] for j in range(KB+1)]
        pf=[t.astype(jnp.float32) for t in pb]
        dp=[dg(t,do,NT) for t in vv]
        delta=functools.reduce(jnp.add,[jnp.sum(a*c,axis=0,keepdims=True) for a,c in zip(pf,dp)])
        ds=[(a*(c-delta)).astype(jnp.bfloat16) for a,c in zip(pf,dp)]
        dq=functools.reduce(jnp.add,[dg(a,c,TN) for a,c in zip(ds,kk)])
        dq_ref[:,cols]=(dq*SCALE).astype(jnp.bfloat16)
        dk_ref[:,cols]=(dg(ds[KB],q,NN)*SCALE).astype(jnp.bfloat16)
        dv_ref[:,cols]=dg(pb[KB],do,NN).astype(jnp.bfloat16)
        for j in range(KB):
            acc[rows[j],cols]+=dg(ds[j],q,NN)
            acc[rows[j],vcols]+=dg(pb[j],do,NN)
    @pl.when(b==pl.num_programs(0)-1)
    def _():
        half=BLK//2
        for i,ref in enumerate((keep_ref,away_ref)):
            for c in range(CB):
                at=slice(c*BLK+i*half,c*BLK+(i+1)*half)
                ref[c*half:(c+1)*half,:width]=(acc[at,:width]*SCALE).astype(jnp.bfloat16)
                ref[c*half:(c+1)*half,width:]=acc[at,width:].astype(jnp.bfloat16)

def bwd(table,place,q,k,v,cache,p,ga,gu,gl):
    T,W=q.shape; heads=W//HD; nb=T//BLK
    blk=pl.BlockSpec((BLK,W),lambda b,t,w:(b,0))
    upper=pl.BlockSpec((BLK,W),lambda b,t,w:(jnp.minimum(b,nb//2-1),0))
    lower=pl.BlockSpec((BLK,W),lambda b,t,w:(jnp.maximum(b-nb//2,0),0))
    full=pl.BlockSpec(cache.shape,lambda b,t,w:(0,0))
    part=pl.BlockSpec((cache.shape[0]//2,cache.shape[1]),lambda b,t,w:(0,0))
    return pl.pallas_call(functools.partial(bwd_kernel,heads),
        grid_spec=pltpu.PrefetchScalarGridSpec(num_scalar_prefetch=2,grid=(nb,),
            in_specs=[blk,blk,blk,full,pl.BlockSpec((1,heads,(KB+1)*BLK,BLK),lambda b,t,w:(b,0,0,0)),blk,upper,lower],
            out_specs=[blk,blk,blk,part,part],
            scratch_shapes=[pltpu.VMEM(cache.shape,jnp.float32)]),
        out_shape=[jax.ShapeDtypeStruct((T,W),jnp.bfloat16)]*3+[jax.ShapeDtypeStruct((cache.shape[0]//2,cache.shape[1]),jnp.bfloat16)]*2,
        compiler_params=pltpu.CompilerParams(vmem_limit_bytes=40<<20),
        cost_estimate=SHORT,
        name="attn_bwd")(table,place,q,k,v,cache,p,ga,gu,gl)


VMEM_LIMIT = 56 << 20


def project_kernel(other, place, *refs):
    w_ref, o_ref = refs[-2:]
    depth = refs[0].shape[1]

    def total(half):
        parts = []
        for j in range(4):
            rows = pl.ds(pl.multiple_of(place[CHUNKS + 4 * other + j] * depth, depth), depth)
            parts.append(dg(refs[2 * j + half][...], w_ref[rows, :], NN))
        return functools.reduce(jnp.add, parts).astype(o_ref.dtype)

    first = pl.program_id(0) < pl.num_programs(0) // 2

    @pl.when(first)
    def _():
        o_ref[...] = total(0)

    @pl.when(jnp.logical_not(first))
    def _():
        o_ref[...] = total(1)


def project(other, place, columns, weight, dtype):
    half, depth = columns[0].shape
    width = weight.shape[1]
    steps = 4
    block = 2 * half // steps
    upper = pl.BlockSpec((block, depth), lambda i, p: (jnp.minimum(i, steps // 2 - 1), 0))
    lower = pl.BlockSpec((block, depth), lambda i, p: (jnp.maximum(i - steps // 2, 0), 0))
    return pl.pallas_call(
        functools.partial(project_kernel, other),
        grid_spec=pltpu.PrefetchScalarGridSpec(
            num_scalar_prefetch=1,
            grid=(steps,),
            in_specs=[upper, lower] * 4 + [pl.BlockSpec((4 * depth, width), lambda i, p: (p[HALF + other], 0))],
            out_specs=pl.BlockSpec((block, width), lambda i, p: (i, 0)),
        ),
        out_shape=jax.ShapeDtypeStruct((2 * half, width), dtype),
        compiler_params=pltpu.CompilerParams(vmem_limit_bytes=VMEM_LIMIT),
        cost_estimate=SHORT,
        name="project",
    )(place, *columns, weight)


def outer_kernel(place, *refs):
    chunks, own, other, rest = refs[:8], refs[8], refs[9], refs[10:]
    picked, attn = rest[-2:]
    half = chunks[0].shape[0]
    width = own.shape[1]
    upper = place[HALF]

    @pl.when(upper == 0)
    def _():
        attn[:, :width] = own[...]
        attn[:, width:] = other[...]

    @pl.when(upper != 0)
    def _():
        attn[:, :width] = other[...]
        attn[:, width:] = own[...]

    for slot in range(4):
        for j in range(4):

            @pl.when(place[SLOTS + slot] == j)
            def _():
                picked[:half, :] = chunks[2 * j][...]
                picked[half:, :] = chunks[2 * j + 1][...]

        out = dg(picked[...], attn[...], TN)
        size = out.shape[0]
        here = slice(slot * size, (slot + 1) * size)
        if len(rest) == 3:
            rest[0][here, :] = out.astype(jnp.bfloat16)
        else:
            out = (out + rest[0][here, :].astype(jnp.float32)).astype(jnp.bfloat16)
            for f in range(2):
                away = f + upper - 2 * f * upper
                to = 4 * f + slot + away * (3 - 2 * slot)
                rest[1][pl.ds(pl.multiple_of(to * size, size), size), :] = out[:, f * width : (f + 1) * width]


def outer(place, columns, own, other, added=None):
    half, depth = columns[0].shape
    width = own.shape[1]
    size = depth // 2
    core = CORE + int(added is None)
    full = pl.BlockSpec(own.shape, lambda i, p: (0, 0))
    both = pl.BlockSpec((4 * size, 2 * width), lambda i, p: (0, 0))
    shape = (4 * size, 2 * width) if added is None else (8 * size, width)
    return pl.pallas_call(
        outer_kernel,
        grid_spec=pltpu.PrefetchScalarGridSpec(
            num_scalar_prefetch=1,
            grid=(1,),
            in_specs=[pl.BlockSpec((half, size), lambda i, p: (0, p[core]))] * 8
            + [full, full]
            + ([] if added is None else [both]),
            out_specs=pl.BlockSpec(shape, lambda i, p: (0, 0)),
            scratch_shapes=[pltpu.VMEM((2 * half, size), jnp.bfloat16), pltpu.VMEM((2 * half, 2 * width), jnp.bfloat16)],
        ),
        out_shape=jax.ShapeDtypeStruct(shape, jnp.bfloat16),
        compiler_params=pltpu.CompilerParams(vmem_limit_bytes=VMEM_LIMIT),
        cost_estimate=SHORT,
        name="outer",
    )(place, *columns, own, other, *([] if added is None else [added]))


AXES = ("row", "col")

def device(xh, y, z, xl, core):
    return (xh * 4 + y) * 16 + (z * 2 + xl) * 2 + core


def every():
    for xh in range(2):
        for y in range(4):
            for z in range(4):
                for xl in range(2):
                    for core in range(2):
                        yield xh, y, z, xl, core


def shifted(xh=0, y=0, z=0, xl=0, core=0):
    return [
        (device(*d), device(d[0] ^ xh, (d[1] + y) % 4, (d[2] + z) % 4, d[3] ^ xl, d[4] ^ core)) for d in every()
    ]


def swap_pairs():
    pairs = []
    for d in every():
        xh, y, z, xl, core = d
        upper, lower = z // 2, z % 2
        away = int(upper != xh)
        pairs.append((device(*d), device(upper, y, xh * 2 + (lower ^ away), xl ^ away, core)))
    return pairs


def place_table():
    rows = []
    for xh, y, z, xl, core in every():
        owners = [(y + step) % 4 for step in STEPS]
        rows.append(
            [xh, 1 - xh, *owners, *(3 - o for o in owners), core, 1 - core, *(owners.index(t) for t in range(4))]
            + [STEPS.index((c // 2 - z) % 4) * 2 + (c % 2 ^ xl) for c in range(CB)]
        )
    return np.array(rows, np.int32)


def send(array, pairs):
    return lax.ppermute(array, AXES, pairs)


def f32(array):
    return array.astype(jnp.float32)


def per_device(grad_out, proj_weight, queries, keys, values, cache_keys, cache_values, block_table):
    bf16 = jnp.bfloat16
    tokens, width = queries.shape
    depth = grad_out.shape[1]
    place = lax.dynamic_index_in_dim(
        jnp.asarray(place_table()), lax.axis_index("row") * 16 + lax.axis_index("col"), keepdims=False
    )
    swap = swap_pairs()
    half = tokens // 2

    rows = cache_keys.shape[0]
    mine = jnp.concatenate([cache_keys, cache_values], axis=1)
    pair = jnp.concatenate([mine, send(mine, shifted(xl=1))], axis=0)

    upper, lower = grad_out[:half], grad_out[half:]
    before_upper, after_lower = send(upper, shifted(y=1)), send(lower, shifted(y=3))
    before_lower, after_upper = send(lower, shifted(y=1)), send(upper, shifted(y=3))
    swapped, before_upper, after_lower, pair, across = lax.optimization_barrier(
        (send(proj_weight, swap), before_upper, after_lower, pair, send(pair, shifted(z=2)))
    )
    near = jnp.concatenate([pair] + [send(pair, shifted(z=4 - STEPS[i])) for i in range(1, 3)] + [across], axis=0)
    near, before_lower, after_upper = lax.optimization_barrier((near, before_lower, after_upper))
    far = send(near, shifted(core=1))
    cache = jnp.stack(
        [near.reshape(CB, rows, 2 * width), far.reshape(CB, rows, 2 * width)], axis=1
    ).reshape(2 * CB * rows, 2 * width)
    weight = lax.all_gather(swapped, "col", axis=0, tiled=True)
    columns = (
        upper,
        lower,
        before_upper,
        before_lower,
        after_upper,
        after_lower,
        send(before_upper, shifted(y=1)),
        send(after_lower, shifted(y=3)),
    )

    attn_out, probs = fwd(block_table, place, queries, keys, values, cache)
    attn_other = send(attn_out, shifted(xh=1))

    other_part, weight = lax.optimization_barrier((project(1, place, columns, weight, bf16), weight))
    own_part = project(0, place, columns, weight, jnp.float32)
    attn_other, own_part = lax.optimization_barrier((attn_other, own_part))
    from_upper, from_lower = send(other_part[:half], shifted(xh=1)), send(other_part[half:], shifted(xh=1))
    theirs = outer(place, columns, attn_out, attn_other)
    theirs, from_upper = lax.optimization_barrier((theirs, from_upper))
    pieces = outer(place, columns, attn_out, attn_other, send(theirs, shifted(core=1)))
    pieces, from_lower, own_part = lax.optimization_barrier((pieces, from_lower, own_part))
    groups = [[2 * i + c for i in range(8)] for c in range(2)]
    pieces = lax.all_to_all(pieces, "col", split_axis=0, concat_axis=0, axis_index_groups=groups, tiled=True)
    total = jnp.sum(f32(pieces.reshape(8, -1, width)), axis=0).astype(bf16)
    grad_weight = send(total, swap)

    grad_q, grad_k, grad_v, keep, away = bwd(
        block_table, place, queries, keys, values, cache, probs, own_part, from_upper, from_lower
    )
    parts = (f32(keep) + f32(send(away, shifted(core=1)))).astype(bf16).reshape(4, 2 * rows, 2 * width)
    parts = sum([f32(parts[0])] + [f32(send(parts[i], shifted(z=STEPS[i]))) for i in range(1, 4)]).astype(bf16)
    total = f32(parts[:rows]) + f32(send(parts[rows:], shifted(xl=1)))
    return (grad_q, grad_k, grad_v, total[:, :width], total[:, width:], grad_weight)


def solution(mesh):
    both = P("col", "row")
    return jax.shard_map(
        per_device, mesh=mesh, in_specs=(both,) * 7 + (P("col", None),), out_specs=(both,) * 6, check_vma=False
    )
```

```python
import functools
import math

import jax
import jax.numpy as jnp
import numpy as np
from jax import lax
from jax.experimental import pallas as pl
from jax.experimental.pallas import tpu as pltpu
from jax.sharding import PartitionSpec as P

HD=128; BLK=128; KB=4; CB=8
SCALE=1.0/math.sqrt(HD); EXPSCALE=SCALE*math.log2(math.e)
SHORT = pl.CostEstimate(flops=1 << 20, bytes_accessed=1 << 16, transcendentals=0)
HALF, CHUNKS, CORE, SLOTS, KEPT = 0, 2, 10, 12, 16
STEPS = (0, 3, 1, 2)
NT=(((1,),(1,)),((),())); TN=(((0,),(0,)),((),())); NN=(((1,),(0,)),((),()))
def dg(a,b,dims): return lax.dot_general(a,b,dims,preferred_element_type=jnp.float32)

def fwd_kernel(heads,table,place,q_ref,k_ref,v_ref,c_ref,o_ref,p_ref):
    b=pl.program_id(0); width=heads*HD
    keyp=lax.broadcasted_iota(jnp.int32,(BLK,BLK),0); qp=lax.broadcasted_iota(jnp.int32,(BLK,BLK),1)
    rows=[pl.ds(pl.multiple_of(place[KEPT+table[b,j]]*BLK,BLK),BLK) for j in range(KB)]
    for h in range(heads):
        cols=slice(h*HD,(h+1)*HD); vcols=slice(width+h*HD,width+(h+1)*HD)
        q=q_ref[:,cols]
        s=[dg(c_ref[r,cols],q,NT) for r in rows]
        s.append(jnp.where(keyp<=qp,dg(k_ref[:,cols],q,NT),-jnp.inf))
        m=functools.reduce(jnp.maximum,[jnp.max(t,axis=0,keepdims=True) for t in s])
        e=[jnp.exp2((t-m)*EXPSCALE) for t in s]
        l=functools.reduce(jnp.add,[jnp.sum(t,axis=0,keepdims=True) for t in e])
        r=1.0/l
        p=[(t*r).astype(jnp.bfloat16) for t in e]
        o=dg(p[KB],v_ref[:,cols],TN)
        for j in range(KB): o=o+dg(p[j],c_ref[rows[j],vcols],TN)
        o_ref[:,cols]=o.astype(jnp.bfloat16)
        for j in range(KB+1): p_ref[0,h,j*BLK:(j+1)*BLK,:]=p[j]

def fwd(table,place,q,k,v,cache):
    T,W=q.shape; heads=W//HD; nb=T//BLK
    blk=pl.BlockSpec((BLK,W),lambda b,t,w:(b,0))
    return pl.pallas_call(functools.partial(fwd_kernel,heads),
        grid_spec=pltpu.PrefetchScalarGridSpec(num_scalar_prefetch=2,grid=(nb,),
            in_specs=[blk,blk,blk,pl.BlockSpec(cache.shape,lambda b,t,w:(0,0))],
            out_specs=[blk,pl.BlockSpec((1,heads,(KB+1)*BLK,BLK),lambda b,t,w:(b,0,0,0))]),
        out_shape=[jax.ShapeDtypeStruct((T,W),jnp.bfloat16),jax.ShapeDtypeStruct((nb,heads,(KB+1)*BLK,BLK),jnp.bfloat16)],
        compiler_params=pltpu.CompilerParams(vmem_limit_bytes=40<<20),
        cost_estimate=SHORT,
        name="attn_fwd")(table,place,q,k,v,cache)

def bwd_kernel(heads,table,place,q_ref,k_ref,v_ref,c_ref,p_ref,ga_ref,gu_ref,gl_ref,dq_ref,dk_ref,dv_ref,keep_ref,away_ref,acc):
    b=pl.program_id(0); width=heads*HD
    @pl.when(b==0)
    def _(): acc[...]=jnp.zeros_like(acc)
    rows=[pl.ds(pl.multiple_of(place[KEPT+table[b,j]]*BLK,BLK),BLK) for j in range(KB)]
    for h in range(heads):
        cols=slice(h*HD,(h+1)*HD); vcols=slice(width+h*HD,width+(h+1)*HD)
        q=q_ref[:,cols]
        gb=jnp.where(b<pl.num_programs(0)//2,gu_ref[:,cols].astype(jnp.float32),gl_ref[:,cols].astype(jnp.float32))
        do=(ga_ref[:,cols]+gb).astype(jnp.bfloat16)
        kk=[c_ref[r,cols] for r in rows]+[k_ref[:,cols]]
        vv=[c_ref[r,vcols] for r in rows]+[v_ref[:,cols]]
        pb=[p_ref[0,h,j*BLK:(j+1)*BLK,:] for j in range(KB+1)]
        pf=[t.astype(jnp.float32) for t in pb]
        dp=[dg(t,do,NT) for t in vv]
        delta=functools.reduce(jnp.add,[jnp.sum(a*c,axis=0,keepdims=True) for a,c in zip(pf,dp)])
        ds=[(a*(c-delta)).astype(jnp.bfloat16) for a,c in zip(pf,dp)]
        dq=functools.reduce(jnp.add,[dg(a,c,TN) for a,c in zip(ds,kk)])
        dq_ref[:,cols]=(dq*SCALE).astype(jnp.bfloat16)
        dk_ref[:,cols]=(dg(ds[KB],q,NN)*SCALE).astype(jnp.bfloat16)
        dv_ref[:,cols]=dg(pb[KB],do,NN).astype(jnp.bfloat16)
        for j in range(KB):
            acc[rows[j],cols]+=dg(ds[j],q,NN)
            acc[rows[j],vcols]+=dg(pb[j],do,NN)
    @pl.when(b==pl.num_programs(0)-1)
    def _():
        half=BLK//2
        for i,ref in enumerate((keep_ref,away_ref)):
            for c in range(CB):
                at=slice(c*BLK+i*half,c*BLK+(i+1)*half)
                ref[c*half:(c+1)*half,:width]=(acc[at,:width]*SCALE).astype(jnp.bfloat16)
                ref[c*half:(c+1)*half,width:]=acc[at,width:].astype(jnp.bfloat16)

def bwd(table,place,q,k,v,cache,p,ga,gu,gl):
    T,W=q.shape; heads=W//HD; nb=T//BLK
    blk=pl.BlockSpec((BLK,W),lambda b,t,w:(b,0))
    upper=pl.BlockSpec((BLK,W),lambda b,t,w:(jnp.minimum(b,nb//2-1),0))
    lower=pl.BlockSpec((BLK,W),lambda b,t,w:(jnp.maximum(b-nb//2,0),0))
    full=pl.BlockSpec(cache.shape,lambda b,t,w:(0,0))
    part=pl.BlockSpec((cache.shape[0]//2,cache.shape[1]),lambda b,t,w:(0,0))
    return pl.pallas_call(functools.partial(bwd_kernel,heads),
        grid_spec=pltpu.PrefetchScalarGridSpec(num_scalar_prefetch=2,grid=(nb,),
            in_specs=[blk,blk,blk,full,pl.BlockSpec((1,heads,(KB+1)*BLK,BLK),lambda b,t,w:(b,0,0,0)),blk,upper,lower],
            out_specs=[blk,blk,blk,part,part],
            scratch_shapes=[pltpu.VMEM(cache.shape,jnp.float32)]),
        out_shape=[jax.ShapeDtypeStruct((T,W),jnp.bfloat16)]*3+[jax.ShapeDtypeStruct((cache.shape[0]//2,cache.shape[1]),jnp.bfloat16)]*2,
        compiler_params=pltpu.CompilerParams(vmem_limit_bytes=40<<20),
        cost_estimate=SHORT,
        name="attn_bwd")(table,place,q,k,v,cache,p,ga,gu,gl)


VMEM_LIMIT = 56 << 20


def project_kernel(other, place, *refs):
    w_ref, o_ref = refs[-2:]
    depth = refs[0].shape[1]

    def total(half):
        parts = []
        for j in range(4):
            rows = pl.ds(pl.multiple_of(place[CHUNKS + 4 * other + j] * depth, depth), depth)
            parts.append(dg(refs[2 * j + half][...], w_ref[rows, :], NN))
        return functools.reduce(jnp.add, parts).astype(o_ref.dtype)

    first = pl.program_id(0) < pl.num_programs(0) // 2

    @pl.when(first)
    def _():
        o_ref[...] = total(0)

    @pl.when(jnp.logical_not(first))
    def _():
        o_ref[...] = total(1)


def project(other, place, columns, weight, dtype):
    half, depth = columns[0].shape
    width = weight.shape[1]
    steps = 4
    block = 2 * half // steps
    upper = pl.BlockSpec((block, depth), lambda i, p: (jnp.minimum(i, steps // 2 - 1), 0))
    lower = pl.BlockSpec((block, depth), lambda i, p: (jnp.maximum(i - steps // 2, 0), 0))
    return pl.pallas_call(
        functools.partial(project_kernel, other),
        grid_spec=pltpu.PrefetchScalarGridSpec(
            num_scalar_prefetch=1,
            grid=(steps,),
            in_specs=[upper, lower] * 4 + [pl.BlockSpec((4 * depth, width), lambda i, p: (p[HALF + other], 0))],
            out_specs=pl.BlockSpec((block, width), lambda i, p: (i, 0)),
        ),
        out_shape=jax.ShapeDtypeStruct((2 * half, width), dtype),
        compiler_params=pltpu.CompilerParams(vmem_limit_bytes=VMEM_LIMIT),
        cost_estimate=SHORT,
        name="project",
    )(place, *columns, weight)


def outer_kernel(place, *refs):
    chunks, own, other, rest = refs[:8], refs[8], refs[9], refs[10:]
    picked, attn = rest[-2:]
    half = chunks[0].shape[0]
    width = own.shape[1]
    upper = place[HALF]

    @pl.when(upper == 0)
    def _():
        attn[:, :width] = own[...]
        attn[:, width:] = other[...]

    @pl.when(upper != 0)
    def _():
        attn[:, :width] = other[...]
        attn[:, width:] = own[...]

    for slot in range(4):
        for j in range(4):

            @pl.when(place[SLOTS + slot] == j)
            def _():
                picked[:half, :] = chunks[2 * j][...]
                picked[half:, :] = chunks[2 * j + 1][...]

        out = dg(picked[...], attn[...], TN)
        size = out.shape[0]
        here = slice(slot * size, (slot + 1) * size)
        if len(rest) == 3:
            rest[0][here, :] = out.astype(jnp.bfloat16)
        else:
            out = (out + rest[0][here, :].astype(jnp.float32)).astype(jnp.bfloat16)
            piece = size // 2
            for f in range(2):
                away = f + upper - 2 * f * upper
                for r in range(2):
                    chunk = slot ^ (2 * r)
                    to = 4 * (upper + r - 2 * r * upper) + chunk + away * (1 - 2 * (chunk % 2))
                    rest[1][pl.ds(pl.multiple_of((2 * to + away) * piece, piece), piece), :] = out[
                        r * piece : (r + 1) * piece, f * width : (f + 1) * width
                    ]


def outer(place, columns, own, other, added=None):
    half, depth = columns[0].shape
    width = own.shape[1]
    size = depth // 2
    core = CORE + int(added is None)
    full = pl.BlockSpec(own.shape, lambda i, p: (0, 0))
    both = pl.BlockSpec((4 * size, 2 * width), lambda i, p: (0, 0))
    shape = (4 * size, 2 * width) if added is None else (8 * size, width)
    return pl.pallas_call(
        outer_kernel,
        grid_spec=pltpu.PrefetchScalarGridSpec(
            num_scalar_prefetch=1,
            grid=(1,),
            in_specs=[pl.BlockSpec((half, size), lambda i, p: (0, p[core]))] * 8
            + [full, full]
            + ([] if added is None else [both]),
            out_specs=pl.BlockSpec(shape, lambda i, p: (0, 0)),
            scratch_shapes=[pltpu.VMEM((2 * half, size), jnp.bfloat16), pltpu.VMEM((2 * half, 2 * width), jnp.bfloat16)],
        ),
        out_shape=jax.ShapeDtypeStruct(shape, jnp.bfloat16),
        compiler_params=pltpu.CompilerParams(vmem_limit_bytes=VMEM_LIMIT),
        cost_estimate=SHORT,
        name="outer",
    )(place, *columns, own, other, *([] if added is None else [added]))


AXES = ("row", "col")

def device(xh, y, z, xl, core):
    return (xh * 4 + y) * 16 + (z * 2 + xl) * 2 + core


def every():
    for xh in range(2):
        for y in range(4):
            for z in range(4):
                for xl in range(2):
                    for core in range(2):
                        yield xh, y, z, xl, core


def shifted(xh=0, y=0, z=0, xl=0, core=0):
    return [
        (device(*d), device(d[0] ^ xh, (d[1] + y) % 4, (d[2] + z) % 4, d[3] ^ xl, d[4] ^ core)) for d in every()
    ]


def swap_pairs():
    pairs = []
    for d in every():
        xh, y, z, xl, core = d
        upper, lower = z // 2, z % 2
        away = int(upper != xh)
        pairs.append((device(*d), device(upper, y, xh * 2 + (lower ^ away), xl ^ away, core)))
    return pairs


def owner_pairs(other, r):
    pairs = []
    for d in every():
        xh, y, z, xl, core = d
        if z // 2 == xh ^ r:
            pairs.append((device(*d), device(xh ^ other, y, xh * 2 + (z % 2 ^ r), xl ^ other, core)))
    return pairs


def place_table():
    rows = []
    for xh, y, z, xl, core in every():
        owners = [(y + step) % 4 for step in STEPS]
        rows.append(
            [xh, 1 - xh, *owners, *(3 - o for o in owners), core, 1 - core, *(owners.index(t) for t in range(4))]
            + [STEPS.index((c // 2 - z) % 4) * 2 + (c % 2 ^ xl) for c in range(CB)]
        )
    return np.array(rows, np.int32)


def send(array, pairs):
    return lax.ppermute(array, AXES, pairs)


def f32(array):
    return array.astype(jnp.float32)


def per_device(grad_out, proj_weight, queries, keys, values, cache_keys, cache_values, block_table):
    bf16 = jnp.bfloat16
    tokens, width = queries.shape
    depth = grad_out.shape[1]
    place = lax.dynamic_index_in_dim(
        jnp.asarray(place_table()), lax.axis_index("row") * 16 + lax.axis_index("col"), keepdims=False
    )
    swap = swap_pairs()
    half = tokens // 2

    rows = cache_keys.shape[0]
    mine = jnp.concatenate([cache_keys, cache_values], axis=1)
    pair = jnp.concatenate([mine, send(mine, shifted(xl=1))], axis=0)

    upper, lower = grad_out[:half], grad_out[half:]
    before_upper, after_lower = send(upper, shifted(y=1)), send(lower, shifted(y=3))
    before_lower, after_upper = send(lower, shifted(y=1)), send(upper, shifted(y=3))
    swapped, before_upper, after_lower, pair, across = lax.optimization_barrier(
        (send(proj_weight, swap), before_upper, after_lower, pair, send(pair, shifted(z=2)))
    )
    near = jnp.concatenate([pair] + [send(pair, shifted(z=4 - STEPS[i])) for i in range(1, 3)] + [across], axis=0)
    near, before_lower, after_upper = lax.optimization_barrier((near, before_lower, after_upper))
    far = send(near, shifted(core=1))
    cache = jnp.stack(
        [near.reshape(CB, rows, 2 * width), far.reshape(CB, rows, 2 * width)], axis=1
    ).reshape(2 * CB * rows, 2 * width)
    weight = lax.all_gather(swapped, "col", axis=0, tiled=True)
    columns = (
        upper,
        lower,
        before_upper,
        before_lower,
        after_upper,
        after_lower,
        send(before_upper, shifted(y=1)),
        send(after_lower, shifted(y=3)),
    )

    attn_out, probs = fwd(block_table, place, queries, keys, values, cache)
    attn_other = send(attn_out, shifted(xh=1))

    other_part, weight = lax.optimization_barrier((project(1, place, columns, weight, bf16), weight))
    own_part = project(0, place, columns, weight, jnp.float32)
    attn_other, own_part = lax.optimization_barrier((attn_other, own_part))
    from_upper, from_lower = send(other_part[:half], shifted(xh=1)), send(other_part[half:], shifted(xh=1))
    theirs = outer(place, columns, attn_out, attn_other)
    theirs, from_upper = lax.optimization_barrier((theirs, from_upper))
    pieces = outer(place, columns, attn_out, attn_other, send(theirs, shifted(core=1)))
    pieces, from_lower, own_part = lax.optimization_barrier((pieces, from_lower, own_part))
    groups = [[2 * i + c for i in range(8)] for c in range(2)]
    pieces = lax.all_to_all(pieces, "col", split_axis=0, concat_axis=0, axis_index_groups=groups, tiled=True)
    total = jnp.sum(f32(pieces.reshape(8, -1, width)), axis=0).astype(bf16)
    own_sum, other_sum = total[: total.shape[0] // 2], total[total.shape[0] // 2 :]
    stays = lax.axis_index("row") // 4 == lax.axis_index("col") // 8
    grad_weight = jnp.concatenate(
        [
            jnp.where(stays, own_sum, send(other_sum, owner_pairs(1, 0))),
            jnp.where(stays, send(own_sum, owner_pairs(0, 1)), send(other_sum, owner_pairs(1, 1))),
        ],
        axis=0,
    )

    grad_q, grad_k, grad_v, keep, away = bwd(
        block_table, place, queries, keys, values, cache, probs, own_part, from_upper, from_lower
    )
    parts = (f32(keep) + f32(send(away, shifted(core=1)))).astype(bf16).reshape(4, 2 * rows, 2 * width)
    parts = sum([f32(parts[0])] + [f32(send(parts[i], shifted(z=STEPS[i]))) for i in range(1, 4)]).astype(bf16)
    total = f32(parts[:rows]) + f32(send(parts[rows:], shifted(xl=1)))
    return (grad_q, grad_k, grad_v, total[:, :width], total[:, width:], grad_weight)


def solution(mesh):
    both = P("col", "row")
    return jax.shard_map(
        per_device, mesh=mesh, in_specs=(both,) * 7 + (P("col", None),), out_specs=(both,) * 6, check_vma=False
    )
```

```python
import functools
import math

import jax
import jax.numpy as jnp
import numpy as np
from jax import lax
from jax.experimental import pallas as pl
from jax.experimental.pallas import tpu as pltpu
from jax.sharding import PartitionSpec as P

HD=128; BLK=128; KB=4; CB=8
SCALE=1.0/math.sqrt(HD); EXPSCALE=SCALE*math.log2(math.e)
SHORT = pl.CostEstimate(flops=1 << 20, bytes_accessed=1 << 16, transcendentals=0)
HALF, CHUNKS, CORE, SLOTS, KEPT = 0, 2, 10, 12, 16
STEPS = (0, 3, 1, 2)
NT=(((1,),(1,)),((),())); TN=(((0,),(0,)),((),())); NN=(((1,),(0,)),((),()))
def dg(a,b,dims): return lax.dot_general(a,b,dims,preferred_element_type=jnp.float32)

def fwd_kernel(heads,table,place,q_ref,k_ref,v_ref,c_ref,o_ref,p_ref):
    b=pl.program_id(0); width=heads*HD
    keyp=lax.broadcasted_iota(jnp.int32,(BLK,BLK),0); qp=lax.broadcasted_iota(jnp.int32,(BLK,BLK),1)
    rows=[pl.ds(pl.multiple_of(place[KEPT+table[b,j]]*BLK,BLK),BLK) for j in range(KB)]
    for h in range(heads):
        cols=slice(h*HD,(h+1)*HD); vcols=slice(width+h*HD,width+(h+1)*HD)
        q=q_ref[:,cols]
        s=[dg(c_ref[r,cols],q,NT) for r in rows]
        s.append(jnp.where(keyp<=qp,dg(k_ref[:,cols],q,NT),-jnp.inf))
        m=functools.reduce(jnp.maximum,[jnp.max(t,axis=0,keepdims=True) for t in s])
        e=[jnp.exp2((t-m)*EXPSCALE) for t in s]
        l=functools.reduce(jnp.add,[jnp.sum(t,axis=0,keepdims=True) for t in e])
        r=1.0/l
        p=[(t*r).astype(jnp.bfloat16) for t in e]
        o=dg(p[KB],v_ref[:,cols],TN)
        for j in range(KB): o=o+dg(p[j],c_ref[rows[j],vcols],TN)
        o_ref[:,cols]=o.astype(jnp.bfloat16)
        for j in range(KB+1): p_ref[0,h,j*BLK:(j+1)*BLK,:]=p[j]

def fwd(table,place,q,k,v,cache):
    T,W=q.shape; heads=W//HD; nb=T//BLK
    blk=pl.BlockSpec((BLK,W),lambda b,t,w:(b,0))
    return pl.pallas_call(functools.partial(fwd_kernel,heads),
        grid_spec=pltpu.PrefetchScalarGridSpec(num_scalar_prefetch=2,grid=(nb,),
            in_specs=[blk,blk,blk,pl.BlockSpec(cache.shape,lambda b,t,w:(0,0))],
            out_specs=[blk,pl.BlockSpec((1,heads,(KB+1)*BLK,BLK),lambda b,t,w:(b,0,0,0))]),
        out_shape=[jax.ShapeDtypeStruct((T,W),jnp.bfloat16),jax.ShapeDtypeStruct((nb,heads,(KB+1)*BLK,BLK),jnp.bfloat16)],
        compiler_params=pltpu.CompilerParams(vmem_limit_bytes=56<<20),
        cost_estimate=SHORT,
        name="attn_fwd")(table,place,q,k,v,cache)

def bwd_kernel(heads,table,place,q_ref,k_ref,v_ref,c_ref,p_ref,ga_ref,gu_ref,gl_ref,dq_ref,dk_ref,dv_ref,keep_ref,away_ref,acc):
    b=pl.program_id(0); width=heads*HD
    @pl.when(b==0)
    def _(): acc[...]=jnp.zeros_like(acc)
    rows=[pl.ds(pl.multiple_of(place[KEPT+table[b,j]]*BLK,BLK),BLK) for j in range(KB)]
    for h in range(heads):
        cols=slice(h*HD,(h+1)*HD); vcols=slice(width+h*HD,width+(h+1)*HD)
        q=q_ref[:,cols]
        gb=jnp.where(b<pl.num_programs(0)//2,gu_ref[:,cols].astype(jnp.float32),gl_ref[:,cols].astype(jnp.float32))
        do=(ga_ref[:,cols]+gb).astype(jnp.bfloat16)
        kk=[c_ref[r,cols] for r in rows]+[k_ref[:,cols]]
        vv=[c_ref[r,vcols] for r in rows]+[v_ref[:,cols]]
        pb=[p_ref[0,h,j*BLK:(j+1)*BLK,:] for j in range(KB+1)]
        pf=[t.astype(jnp.float32) for t in pb]
        dp=[dg(t,do,NT) for t in vv]
        delta=functools.reduce(jnp.add,[jnp.sum(a*c,axis=0,keepdims=True) for a,c in zip(pf,dp)])
        ds=[(a*(c-delta)).astype(jnp.bfloat16) for a,c in zip(pf,dp)]
        dq=functools.reduce(jnp.add,[dg(a,c,TN) for a,c in zip(ds,kk)])
        dq_ref[:,cols]=(dq*SCALE).astype(jnp.bfloat16)
        dk_ref[:,cols]=(dg(ds[KB],q,NN)*SCALE).astype(jnp.bfloat16)
        dv_ref[:,cols]=dg(pb[KB],do,NN).astype(jnp.bfloat16)
        for j in range(KB):
            acc[rows[j],cols]+=dg(ds[j],q,NN)
            acc[rows[j],vcols]+=dg(pb[j],do,NN)
    @pl.when(b==pl.num_programs(0)-1)
    def _():
        half=BLK//2
        for i,ref in enumerate((keep_ref,away_ref)):
            for c in range(CB):
                at=slice(c*BLK+i*half,c*BLK+(i+1)*half)
                ref[c*half:(c+1)*half,:width]=(acc[at,:width]*SCALE).astype(jnp.bfloat16)
                ref[c*half:(c+1)*half,width:]=acc[at,width:].astype(jnp.bfloat16)

def bwd(table,place,q,k,v,cache,p,ga,gu,gl):
    T,W=q.shape; heads=W//HD; nb=T//BLK
    blk=pl.BlockSpec((BLK,W),lambda b,t,w:(b,0))
    upper=pl.BlockSpec((BLK,W),lambda b,t,w:(jnp.minimum(b,nb//2-1),0))
    lower=pl.BlockSpec((BLK,W),lambda b,t,w:(jnp.maximum(b-nb//2,0),0))
    full=pl.BlockSpec(cache.shape,lambda b,t,w:(0,0))
    part=pl.BlockSpec((cache.shape[0]//2,cache.shape[1]),lambda b,t,w:(0,0))
    return pl.pallas_call(functools.partial(bwd_kernel,heads),
        grid_spec=pltpu.PrefetchScalarGridSpec(num_scalar_prefetch=2,grid=(nb,),
            in_specs=[blk,blk,blk,full,pl.BlockSpec((1,heads,(KB+1)*BLK,BLK),lambda b,t,w:(b,0,0,0)),blk,upper,lower],
            out_specs=[blk,blk,blk,part,part],
            scratch_shapes=[pltpu.VMEM(cache.shape,jnp.float32)]),
        out_shape=[jax.ShapeDtypeStruct((T,W),jnp.bfloat16)]*3+[jax.ShapeDtypeStruct((cache.shape[0]//2,cache.shape[1]),jnp.bfloat16)]*2,
        compiler_params=pltpu.CompilerParams(vmem_limit_bytes=56<<20),
        cost_estimate=SHORT,
        name="attn_bwd")(table,place,q,k,v,cache,p,ga,gu,gl)


VMEM_LIMIT = 56 << 20


def project_kernel(other, place, *refs):
    w_ref, o_ref = refs[-2:]
    depth = refs[0].shape[1]

    def total(half):
        parts = []
        for j in range(4):
            rows = pl.ds(pl.multiple_of(place[CHUNKS + 4 * other + j] * depth, depth), depth)
            parts.append(dg(refs[2 * j + half][...], w_ref[rows, :], NN))
        return functools.reduce(jnp.add, parts).astype(o_ref.dtype)

    first = pl.program_id(0) < pl.num_programs(0) // 2

    @pl.when(first)
    def _():
        o_ref[...] = total(0)

    @pl.when(jnp.logical_not(first))
    def _():
        o_ref[...] = total(1)


def project(other, place, columns, weight, dtype):
    half, depth = columns[0].shape
    width = weight.shape[1]
    steps = 4
    block = 2 * half // steps
    upper = pl.BlockSpec((block, depth), lambda i, p: (jnp.minimum(i, steps // 2 - 1), 0))
    lower = pl.BlockSpec((block, depth), lambda i, p: (jnp.maximum(i - steps // 2, 0), 0))
    return pl.pallas_call(
        functools.partial(project_kernel, other),
        grid_spec=pltpu.PrefetchScalarGridSpec(
            num_scalar_prefetch=1,
            grid=(steps,),
            in_specs=[upper, lower] * 4 + [pl.BlockSpec((4 * depth, width), lambda i, p: (p[HALF + other], 0))],
            out_specs=pl.BlockSpec((block, width), lambda i, p: (i, 0)),
        ),
        out_shape=jax.ShapeDtypeStruct((2 * half, width), dtype),
        compiler_params=pltpu.CompilerParams(vmem_limit_bytes=VMEM_LIMIT),
        cost_estimate=SHORT,
        name="project",
    )(place, *columns, weight)


def outer_kernel(place, *refs):
    chunks, own, other, rest = refs[:8], refs[8], refs[9], refs[10:]
    picked, attn = rest[-2:]
    half = chunks[0].shape[0]
    width = own.shape[1]
    upper = place[HALF]

    @pl.when(upper == 0)
    def _():
        attn[:, :width] = own[...]
        attn[:, width:] = other[...]

    @pl.when(upper != 0)
    def _():
        attn[:, :width] = other[...]
        attn[:, width:] = own[...]

    for slot in range(4):
        for j in range(4):

            @pl.when(place[SLOTS + slot] == j)
            def _():
                picked[:half, :] = chunks[2 * j][...]
                picked[half:, :] = chunks[2 * j + 1][...]

        out = dg(picked[...], attn[...], TN)
        size = out.shape[0]
        here = slice(slot * size, (slot + 1) * size)
        if len(rest) == 3:
            rest[0][here, :] = out.astype(jnp.bfloat16)
        else:
            out = (out + rest[0][here, :].astype(jnp.float32)).astype(jnp.bfloat16)
            piece = size // 2
            for f in range(2):
                away = f + upper - 2 * f * upper
                for r in range(2):
                    chunk = slot ^ (2 * r)
                    to = 4 * (upper + r - 2 * r * upper) + chunk + away * (1 - 2 * (chunk % 2))
                    rest[1][pl.ds(pl.multiple_of((2 * to + away) * piece, piece), piece), :] = out[
                        r * piece : (r + 1) * piece, f * width : (f + 1) * width
                    ]


def outer(place, columns, own, other, added=None):
    half, depth = columns[0].shape
    width = own.shape[1]
    size = depth // 2
    core = CORE + int(added is None)
    full = pl.BlockSpec(own.shape, lambda i, p: (0, 0))
    both = pl.BlockSpec((4 * size, 2 * width), lambda i, p: (0, 0))
    shape = (4 * size, 2 * width) if added is None else (8 * size, width)
    return pl.pallas_call(
        outer_kernel,
        grid_spec=pltpu.PrefetchScalarGridSpec(
            num_scalar_prefetch=1,
            grid=(1,),
            in_specs=[pl.BlockSpec((half, size), lambda i, p: (0, p[core]))] * 8
            + [full, full]
            + ([] if added is None else [both]),
            out_specs=pl.BlockSpec(shape, lambda i, p: (0, 0)),
            scratch_shapes=[pltpu.VMEM((2 * half, size), jnp.bfloat16), pltpu.VMEM((2 * half, 2 * width), jnp.bfloat16)],
        ),
        out_shape=jax.ShapeDtypeStruct(shape, jnp.bfloat16),
        compiler_params=pltpu.CompilerParams(vmem_limit_bytes=VMEM_LIMIT),
        cost_estimate=SHORT,
        name="outer",
    )(place, *columns, own, other, *([] if added is None else [added]))


AXES = ("row", "col")

def device(xh, y, z, xl, core):
    return (xh * 4 + y) * 16 + (z * 2 + xl) * 2 + core


def every():
    for xh in range(2):
        for y in range(4):
            for z in range(4):
                for xl in range(2):
                    for core in range(2):
                        yield xh, y, z, xl, core


def shifted(xh=0, y=0, z=0, xl=0, core=0):
    return [
        (device(*d), device(d[0] ^ xh, (d[1] + y) % 4, (d[2] + z) % 4, d[3] ^ xl, d[4] ^ core)) for d in every()
    ]


def swap_pairs():
    pairs = []
    for d in every():
        xh, y, z, xl, core = d
        upper, lower = z // 2, z % 2
        away = int(upper != xh)
        pairs.append((device(*d), device(upper, y, xh * 2 + (lower ^ away), xl ^ away, core)))
    return pairs


def owner_pairs(other, r):
    pairs = []
    for d in every():
        xh, y, z, xl, core = d
        if z // 2 == xh ^ r:
            pairs.append((device(*d), device(xh ^ other, y, xh * 2 + (z % 2 ^ r), xl ^ other, core)))
    return pairs


def place_table():
    rows = []
    for xh, y, z, xl, core in every():
        owners = [(y + step) % 4 for step in STEPS]
        rows.append(
            [xh, 1 - xh, *owners, *(3 - o for o in owners), core, 1 - core, *(owners.index(t) for t in range(4))]
            + [STEPS.index((c // 2 - z) % 4) * 2 + (c % 2 ^ xl) for c in range(CB)]
        )
    return np.array(rows, np.int32)


def send(array, pairs):
    return lax.ppermute(array, AXES, pairs)


def f32(array):
    return array.astype(jnp.float32)


def per_device(grad_out, proj_weight, queries, keys, values, cache_keys, cache_values, block_table):
    bf16 = jnp.bfloat16
    tokens, width = queries.shape
    depth = grad_out.shape[1]
    place = lax.dynamic_index_in_dim(
        jnp.asarray(place_table()), lax.axis_index("row") * 16 + lax.axis_index("col"), keepdims=False
    )
    swap = swap_pairs()
    half = tokens // 2

    rows = cache_keys.shape[0]
    mine = jnp.concatenate([cache_keys, cache_values], axis=1)
    pair = jnp.concatenate([mine, send(mine, shifted(xl=1))], axis=0)

    upper, lower = grad_out[:half], grad_out[half:]
    before_upper, after_lower = send(upper, shifted(y=1)), send(lower, shifted(y=3))
    before_lower, after_upper = send(lower, shifted(y=1)), send(upper, shifted(y=3))
    swapped, before_upper, after_lower, pair, across = lax.optimization_barrier(
        (send(proj_weight, swap), before_upper, after_lower, pair, send(pair, shifted(z=2)))
    )
    near = jnp.concatenate([pair] + [send(pair, shifted(z=4 - STEPS[i])) for i in range(1, 3)] + [across], axis=0)
    near, before_lower, after_upper = lax.optimization_barrier((near, before_lower, after_upper))
    far = send(near, shifted(core=1))
    cache = jnp.stack(
        [near.reshape(CB, rows, 2 * width), far.reshape(CB, rows, 2 * width)], axis=1
    ).reshape(2 * CB * rows, 2 * width)
    weight = lax.all_gather(swapped, "col", axis=0, tiled=True)
    columns = (
        upper,
        lower,
        before_upper,
        before_lower,
        after_upper,
        after_lower,
        send(before_upper, shifted(y=1)),
        send(after_lower, shifted(y=3)),
    )

    attn_out, probs = fwd(block_table, place, queries, keys, values, cache)
    attn_other = send(attn_out, shifted(xh=1))

    other_part, weight = lax.optimization_barrier((project(1, place, columns, weight, bf16), weight))
    own_part = project(0, place, columns, weight, jnp.float32)
    attn_other, own_part = lax.optimization_barrier((attn_other, own_part))
    from_upper, from_lower = send(other_part[:half], shifted(xh=1)), send(other_part[half:], shifted(xh=1))
    theirs = outer(place, columns, attn_out, attn_other)
    theirs, from_upper = lax.optimization_barrier((theirs, from_upper))
    pieces = outer(place, columns, attn_out, attn_other, send(theirs, shifted(core=1)))
    pieces, from_lower, own_part = lax.optimization_barrier((pieces, from_lower, own_part))
    groups = [[2 * i + c for i in range(8)] for c in range(2)]
    pieces = lax.all_to_all(pieces, "col", split_axis=0, concat_axis=0, axis_index_groups=groups, tiled=True)
    total = jnp.sum(f32(pieces.reshape(8, -1, width)), axis=0).astype(bf16)
    own_sum, other_sum = total[: total.shape[0] // 2], total[total.shape[0] // 2 :]
    stays = lax.axis_index("row") // 4 == lax.axis_index("col") // 8
    grad_weight = jnp.concatenate(
        [
            jnp.where(stays, own_sum, send(other_sum, owner_pairs(1, 0))),
            jnp.where(stays, send(own_sum, owner_pairs(0, 1)), send(other_sum, owner_pairs(1, 1))),
        ],
        axis=0,
    )

    grad_q, grad_k, grad_v, keep, away = bwd(
        block_table, place, queries, keys, values, cache, probs, own_part, from_upper, from_lower
    )
    parts = (f32(keep) + f32(send(away, shifted(core=1)))).astype(bf16).reshape(4, 2 * rows, 2 * width)
    parts = sum([f32(parts[0])] + [f32(send(parts[i], shifted(z=STEPS[i]))) for i in range(1, 4)]).astype(bf16)
    total = f32(parts[:rows]) + f32(send(parts[rows:], shifted(xl=1)))
    return (grad_q, grad_k, grad_v, total[:, :width], total[:, width:], grad_weight)


def solution(mesh):
    both = P("col", "row")
    return jax.shard_map(
        per_device, mesh=mesh, in_specs=(both,) * 7 + (P("col", None),), out_specs=(both,) * 6, check_vma=False
    )
```
